32 devices in a mesh: groups: 2 (over y), ctx: 4 (over z), exp: 2 (over x), tp: 2 (over core).
Axes of the slice: x: 2, y: 2, z: 4, core: 2. Of those that a mesh axis runs over, the one named last changes fastest.
Arguments:
- tokens: bfloat16 [1024, 3072], P(('groups', 'ctx')), parts along dimension 0, may hold values from -6 to 6
- out_grad: bfloat16 [1024, 3072], P(('groups', 'ctx')), parts along dimension 0, may hold values from -6 to 6
- expert_ids: int32 [1024, 2], P(('groups', 'ctx')), parts along dimension 0, may hold values from 0 to 3, all different within a row; in each aligned block of 128 rows (0 to 127, 128 to 255, ...) at most 72 rows name the same one
- gate_weights: float32 [1024, 2], P(('groups', 'ctx')), parts along dimension 0, may hold values from 0.1 to 1
- gate_matrix: bfloat16 [4, 3072, 8192], P('exp', None, ('ctx', 'tp')), may hold values from -0.109375 to 0.109375
- up_matrix: bfloat16 [4, 3072, 8192], P('exp', None, ('ctx', 'tp')), may hold values from -0.109375 to 0.109375
- down_matrix: bfloat16 [4, 8192, 3072], P('exp', ('ctx', 'tp')), may hold values from -0.0625 to 0.0625
Outputs:
- grad_gate: bfloat16 [8, 3072, 8192], P(('groups', 'exp'), None, ('ctx', 'tp')), parts along dimension 0
- grad_up: bfloat16 [8, 3072, 8192], P(('groups', 'exp'), None, ('ctx', 'tp')), parts along dimension 0
- grad_down: bfloat16 [8, 8192, 3072], P(('groups', 'exp'), ('ctx', 'tp')), parts along dimension 0
- grad_tokens: bfloat16 [1024, 3072], P(('groups', 'ctx'), ('exp', 'tp')), parts along dimension 0
The draws below stay inside these ranges and needn't reach their ends.
There are 2 independent parts, one for each index of `groups`. The reference program is written for one: setup_inputs(seed, part) draws one part's arguments, and reference() takes and returns one part's arrays. A program takes and returns all parts, laid end to end along the dimension named above; an argument that names none is the same for every part. Nothing has to cross between parts.
Inputs may be any that keep to these rules, and one draw needn't show every extreme that they name: `expert_ids`: the 2 experts of a token differ; among the 128 tokens of one aligned block at most 72 name any one expert.
All inputs are finite; a program needn't handle non-finite values.
Results may differ from the reference program's by a relative error of at most 0.014.
Values may be sent and summed in bfloat16 or wider, within the bound.
No kernel may reach another device: no remote copies, remote signals or barrier semaphores. Data moves between devices by JAX's collectives and lax.ppermute only.
A program may use at most 192 MiB of HBM per device.

```python
import math
import jax
import jax.numpy as jnp
import numpy as np
from jax import lax

D = 3072
FF = 8192
EXPERTS = 4
TOP = 2
TOK_DEV = 128
CAP = 72
TOKENS = 512
N_CTX = 4
N_TP = 2


def shard_levels(rng, shape, shards, least, largest):
    gain = 1.0
    for position, blocks in shards:
        draws = jax.random.uniform(jax.random.fold_in(jax.random.fold_in(rng, 6), position), (blocks,), jnp.float32, least / len(shards), largest / len(shards))
        gain = gain * jnp.repeat(jnp.exp(draws), shape[position] // blocks).reshape((-1,) + (1,) * (len(shape) - 1 - position))
    return gain


def assign_block(own_key, own, number, rows, amount, top, reach, lean):
    sequence = jax.random.permutation(own_key, amount)
    heavy_load, usual = portions_of(amount, rows * top, reach, lean, True), portions_of(amount, rows * top, reach, lean, False)
    places = jnp.arange(amount)

    def named(sizes, offset_by):
        used = int((sizes > 0).sum())
        fixed = max(1, used // 4)
        moved = fixed + (places - fixed + offset_by * (used - fixed)) % max(1, amount - fixed)
        return jnp.zeros((amount,), jnp.int32).at[sequence[jnp.where(places < fixed, places, moved)]].set(jnp.asarray(sizes, jnp.int32))

    sizes = jnp.where(number % 4 == 0, named(heavy_load, number // 4), named(usual, number - number // 4 - 1))
    mixed = jax.random.permutation(jax.random.fold_in(own, 3), amount)
    giver, receiver = mixed[0:amount // 2 * 2:2], mixed[1:amount // 2 * 2:2]
    room = jnp.minimum(sizes[giver] - 1, reach - sizes[receiver]) // 2
    room = jnp.where((giver == sequence[0]) | (receiver == sequence[0]) | (sizes[receiver] == 0), 0, jnp.maximum(room, 0))
    moved = jax.random.randint(jax.random.fold_in(own, 4), (amount // 2,), 0, 1 << 20) % (room + 1)
    sizes = sizes.at[giver].add(-moved).at[receiver].add(moved)
    labels = jnp.searchsorted(jnp.cumsum(sizes), jnp.arange(rows * top), side="right").astype(jnp.int32)
    table = labels.reshape(top, rows).T
    table = table[jax.random.permutation(jax.random.fold_in(own, 1), rows)]
    offset_by = jax.random.randint(jax.random.fold_in(own, 2), (rows, 1), 0, top)
    return jnp.take_along_axis(table, (jnp.arange(top)[None, :] + offset_by) % top, axis=1)


def portions_of(amount, total, bound, lean, full):
    portions = [(1 << 20) // math.isqrt(grade ** lean) + 1 for grade in range(1, amount + 1)]
    largest = bound if full else min(bound, max(-(-total // amount), total * portions[0] // sum(portions)))
    least = 1 if total - largest >= amount - 1 else 0
    counts, spare = [largest] + [least] * (amount - 1), total - largest - least * (amount - 1)
    while spare > 0:
        movable = [i for i in range(1, amount) if counts[i] < largest] or [i for i in range(1, amount) if counts[i] < bound]
        whole, left = sum([portions[i] for i in movable]), spare
        for i in movable:
            addition = min(bound - counts[i], max(1, left * portions[i] // whole), spare)
            counts[i] = counts[i] + addition
            spare = spare - addition
    return np.array(counts)


def noise(own_key, shape, spread, limit, split=(), held_as=jnp.bfloat16):
    array = spread * jax.random.normal(own_key, shape, jnp.float32)
    if split:
        array = array * shard_levels(own_key, shape, split, -0.22, 0.18)
    return jnp.clip(array, -limit, limit).astype(held_as)


def setup_inputs(seed: int = 0, part: int = 0) -> dict:
    streams_of = jax.random.split(jax.random.key(seed), 8)
    own_keys = jax.random.split(jax.random.fold_in(streams_of[7], part), 8)
    tokens = noise(own_keys[0], (TOKENS, D), 1.0, 6.0, ((0, 4),))
    out_grad = noise(own_keys[1], (TOKENS, D), 1.0, 6.0, ((0, 4),))
    expert_ids_keys = jax.random.split(jax.random.fold_in(own_keys[2], 1), TOKENS // TOK_DEV)
    expert_ids_turns = jax.random.permutation(jax.random.fold_in(own_keys[2], 3), TOKENS // TOK_DEV)
    expert_ids = jax.vmap(lambda own, number: assign_block(jax.random.fold_in(own_keys[2], 2), own, number, TOK_DEV, EXPERTS, TOP, CAP, 2))(expert_ids_keys, expert_ids_turns).reshape((TOKENS, TOP))
    gate_weights = jnp.clip(0.1 + 0.9 * jax.random.uniform(own_keys[3], (TOKENS, TOP), jnp.float32) ** shard_levels(own_keys[3], (TOKENS, TOP), ((0, 4),), -0.2, 0.2), 0.1, 1.0)
    gate_matrix = noise(streams_of[4], (EXPERTS, D, FF), D ** -0.5, 0.109375, ((0, 2), (2, 8)))
    up_matrix = noise(streams_of[5], (EXPERTS, D, FF), D ** -0.5, 0.109375, ((0, 2), (2, 8)))
    down_matrix = noise(streams_of[6], (EXPERTS, FF, D), FF ** -0.5, 0.0625, ((0, 2), (1, 8)))
    return {"tokens": tokens, "out_grad": out_grad, "expert_ids": expert_ids, "gate_weights": gate_weights, "gate_matrix": gate_matrix, "up_matrix": up_matrix, "down_matrix": down_matrix}


def pack_block(block_ids, block_gates, block_tokens, block_grads, expert):
    rows_here = block_tokens.shape[0]
    chosen = block_ids == expert
    member = jnp.any(chosen, axis=1)
    weight = jnp.sum(jnp.where(chosen, block_gates, jnp.zeros_like(block_gates)), axis=1)
    order_index = (jnp.cumsum(member.astype(jnp.int32)) - 1).astype(jnp.int32)
    slot_ids = jnp.arange(CAP, dtype=jnp.int32)
    positions = jnp.arange(rows_here, dtype=jnp.int32)
    match = jnp.logical_and(member[None, :], order_index[None, :] == slot_ids[:, None])
    filled = jnp.any(match, axis=1)
    source = jnp.sum(jnp.where(match, positions[None, :], 0), axis=1).astype(jnp.int32)
    source = source + jnp.where(filled, 0, rows_here).astype(jnp.int32)
    scaled = (weight[:, None] * block_grads.astype(jnp.float32)).astype(jnp.bfloat16)
    zero_row = jnp.zeros((1, block_tokens.shape[1]), jnp.bfloat16)
    packed_tokens = jnp.take(jnp.concatenate([block_tokens, zero_row], axis=0), source, axis=0)
    packed_grads = jnp.take(jnp.concatenate([scaled, zero_row], axis=0), source, axis=0)
    home_slot = jnp.where(member, order_index, CAP).astype(jnp.int32)
    return packed_tokens, packed_grads, home_slot


def sliced_rows(gate_grad, up_grad, gate_matrix, up_matrix):
    slices = N_CTX * N_TP
    width = FF // slices
    rows = gate_grad.shape[0]
    gate_g = gate_grad.reshape(rows, slices, width).transpose(1, 0, 2)
    up_g = up_grad.reshape(rows, slices, width).transpose(1, 0, 2)
    gate_m = gate_matrix.reshape(D, slices, width).transpose(1, 0, 2)
    up_m = up_matrix.reshape(D, slices, width).transpose(1, 0, 2)

    def add_slice(total, item):
        g_part, u_part, gm_part, um_part = item
        term = jnp.dot(g_part, gm_part.T, preferred_element_type=jnp.float32)
        term = term + jnp.dot(u_part, um_part.T, preferred_element_type=jnp.float32)
        rounded = lax.optimization_barrier(term.astype(jnp.bfloat16))
        return total + rounded.astype(jnp.float32), None

    total, unused = lax.scan(add_slice, jnp.zeros((rows, D), jnp.float32), (gate_g, up_g, gate_m, up_m))
    return total


def expert_backward(packed_tokens, packed_grads, gate_matrix, up_matrix, down_matrix):
    gate_pre = jnp.dot(packed_tokens, gate_matrix, preferred_element_type=jnp.float32)
    up_pre = jnp.dot(packed_tokens, up_matrix, preferred_element_type=jnp.float32)
    sig = jax.nn.sigmoid(gate_pre)
    act = gate_pre * sig
    hidden = (act * up_pre).astype(jnp.bfloat16)
    hidden_grad = jnp.dot(packed_grads, down_matrix.T, preferred_element_type=jnp.float32)
    up_grad = (hidden_grad * act).astype(jnp.bfloat16)
    gate_grad = (hidden_grad * up_pre * sig * (1.0 + gate_pre * (1.0 - sig))).astype(jnp.bfloat16)
    grad_down = jnp.dot(hidden.T, packed_grads, preferred_element_type=jnp.float32).astype(jnp.bfloat16)
    grad_gate = jnp.dot(packed_tokens.T, gate_grad, preferred_element_type=jnp.float32).astype(jnp.bfloat16)
    grad_up = jnp.dot(packed_tokens.T, up_grad, preferred_element_type=jnp.float32).astype(jnp.bfloat16)
    row_grads = sliced_rows(gate_grad, up_grad, gate_matrix, up_matrix)
    return grad_gate, grad_up, grad_down, row_grads


def reference(tokens, out_grad, expert_ids, gate_weights, gate_matrix, up_matrix, down_matrix):
    blocks = TOKENS // TOK_DEV
    token_blocks = tokens.reshape(blocks, TOK_DEV, D)
    grad_blocks = out_grad.reshape(blocks, TOK_DEV, D)
    id_blocks = expert_ids.reshape(blocks, TOK_DEV, TOP)
    weight_blocks = gate_weights.reshape(blocks, TOK_DEV, TOP)

    def one_expert(item):
        expert, gate_part, up_part, down_part = item

        def pack_one(block_ids, block_gates, block_tokens, block_grads):
            return pack_block(block_ids, block_gates, block_tokens, block_grads, expert)

        packed_tokens, packed_grads, home_slot = jax.vmap(pack_one)(id_blocks, weight_blocks, token_blocks, grad_blocks)
        grad_gate, grad_up, grad_down, row_grads = expert_backward(
            packed_tokens.reshape(blocks * CAP, D), packed_grads.reshape(blocks * CAP, D),
            gate_part, up_part, down_part)
        row_grads = row_grads.reshape(blocks, CAP, D)
        padded = jnp.concatenate([row_grads, jnp.zeros((blocks, 1, D), jnp.float32)], axis=1)
        placed = jax.vmap(lambda rows, slots: jnp.take(rows, slots, axis=0))(padded, home_slot)
        return grad_gate, grad_up, grad_down, placed.reshape(TOKENS, D)

    grad_gate, grad_up, grad_down, placed = lax.map(
        one_expert, (jnp.arange(EXPERTS, dtype=jnp.int32), gate_matrix, up_matrix, down_matrix))
    grad_tokens = jnp.sum(placed, axis=0).astype(jnp.bfloat16)
    return grad_gate, grad_up, grad_down, grad_tokens
```

```python
import functools

import jax
import jax.numpy as jnp
from jax import lax
from jax.experimental import pallas as pl
from jax.experimental.pallas import tpu as pltpu
from jax.sharding import PartitionSpec as P

CAP = 72
VMEM_LIMIT = 56 * 1024 * 1024
F32 = jnp.float32
BF16 = jnp.bfloat16
NN = (((1,), (0,)), ((), ()))
NT = (((1,), (1,)), ((), ()))
TN = (((0,), (0,)), ((), ()))


def mm(a, b, dims):
    return lax.dot_general(a, b, dims, preferred_element_type=F32)


def params():
    return pltpu.CompilerParams(vmem_limit_bytes=VMEM_LIMIT)


def cost(flops, nbytes):
    return pl.CostEstimate(flops=int(flops), bytes_accessed=int(nbytes), transcendentals=0)


def whole(shape):
    return pl.BlockSpec(shape, lambda *_: (0,) * len(shape))


def shift(count, by):
    return [(i, (i + by) % count) for i in range(count)]


def pair_rows(metas, row, pair):
    first = metas[2 * pair][pl.ds(row, 1), :]
    second = metas[2 * pair + 1][pl.ds(row, 1), :]
    return first, second


def pair_one_hot(metas, expert, pair):
    first, second = pair_rows(metas, expert, pair)
    second = jnp.where(second >= 0, second + CAP, second)
    slot = jnp.concatenate([first, second], axis=1)
    rows = lax.broadcasted_iota(jnp.int32, (2 * CAP, slot.shape[1]), 0).astype(F32)
    return rows == slot


class Gathered:
    def __init__(self, refs, exp_count):
        self.own = refs[0]
        self.slabs = [(dx, dc, refs[1 + dx * 2 + dc]) for dx in range(exp_count) for dc in range(2)]

    def pack(self, here, exp_count, width, pair, hot, scale, store):
        for dx, dc, ref in self.slabs:
            x = lax.rem(here[0] + exp_count - dx, exp_count)
            c = lax.rem(here[1] + dc, 2)
            column = pl.multiple_of((x * 2 + c) * width, 128)
            if pair == 0:
                rows = jnp.concatenate([self.own[:, pl.ds(column, width)], ref[0]], axis=0)
            else:
                rows = jnp.concatenate([ref[2 * pair - 1], ref[2 * pair]], axis=0)
            packed = mm(hot, rows, NN)
            if scale is not None:
                packed = packed * scale
            store(column, packed.astype(BF16))


def forward_kernel(n, exp_count, width, here_ref, *refs):
    count = 1 + 2 * exp_count
    data = Gathered(refs[:count], exp_count)
    metas = refs[count:count + n]
    gate_w, up_w, xp_ref, hid_ref, act_ref, dact_ref = refs[count + n:]
    local = pl.program_id(0)
    here = (here_ref[0], here_ref[1])
    expert = here[0] * pl.num_programs(0) + local

    @pl.when(pl.program_id(1) == 0)
    def _():
        for pair in range(n // 2):
            hot = pair_one_hot(metas, expert, pair).astype(BF16)

            def store(column, value):
                xp_ref[local, pl.ds(pair * 2 * CAP, 2 * CAP), pl.ds(column, width)] = value

            data.pack(here, exp_count, width, pair, hot, None, store)

    rows = xp_ref[local]
    gate = mm(rows, gate_w[0], NN)
    up = mm(rows, up_w[0], NN)
    sig = jax.nn.sigmoid(gate)
    act = gate * sig
    hid_ref[0] = (act * up).astype(BF16)
    act_ref[0] = act
    dact_ref[0] = up * sig * (1.0 + gate * (1.0 - sig))


def hidden_kernel(n, exp_count, width, experts, here_ref, *refs):
    count = 1 + 2 * exp_count
    data = Gathered(refs[:count], exp_count)
    metas = refs[count:count + n]
    down_w, act_ref, dact_ref, gp_ref, gg_ref, ug_ref = refs[count + n:]
    local = pl.program_id(0)
    here = (here_ref[0], here_ref[1])
    expert = here[0] * pl.num_programs(0) + local

    @pl.when(pl.program_id(1) == 0)
    def _():
        for pair in range(n // 2):
            hot = pair_one_hot(metas, expert, pair)
            weights = jnp.concatenate(pair_rows(metas, experts + expert, pair), axis=1)
            scale = jnp.sum(jnp.where(hot, weights, 0.0), axis=1, keepdims=True)

            def store(column, value):
                gp_ref[local, pl.ds(pair * 2 * CAP, 2 * CAP), pl.ds(column, width)] = value

            data.pack(here, exp_count, width, pair, hot.astype(BF16), scale, store)

    hidden_grad = mm(gp_ref[local], down_w[0], NT)
    ug_ref[0] = (hidden_grad * act_ref[0]).astype(BF16)
    gg_ref[0] = (hidden_grad * dact_ref[0]).astype(BF16)


def rows_kernel(n, local_count, has_add, pick_ref, here_ref, *refs):
    del pick_ref
    metas = refs[:n]
    gg_ref, ug_ref, gate_w, up_w = refs[n:n + 4]
    add_ref = refs[n + 4] if has_add else None
    out_ref = refs[-1]
    terms = []
    for local in range(local_count):
        expert = here_ref[0] * local_count + local
        term = mm(gg_ref[local], gate_w[local], NT) + mm(ug_ref[local], up_w[local], NT)
        terms.append((expert, term.astype(BF16)))
    for pair in range(n // 2):
        total = None
        for expert, term in terms:
            hot = pair_one_hot(metas, expert, pair).astype(BF16)
            part = mm(hot, term[pair * 2 * CAP:(pair + 1) * 2 * CAP], TN)
            total = part if total is None else total + part
        half = total.shape[0] // 2
        for k in range(2):
            block = total[k * half:(k + 1) * half]
            if has_add:
                block = block + add_ref[2 * pair + k].astype(F32)
            out_ref[2 * pair + k] = block.astype(BF16)


def outer_kernel(a_ref, b_ref, out_ref):
    out_ref[0] = mm(a_ref[0], b_ref[0], TN).astype(BF16)


def weight_grad(a, b):
    experts, slots, m = a.shape
    cols = b.shape[2]
    tile = min(512, m)
    return pl.pallas_call(
        outer_kernel,
        out_shape=jax.ShapeDtypeStruct((experts, m, cols), BF16),
        grid=(experts, m // tile),
        in_specs=[
            pl.BlockSpec((1, slots, tile), lambda e, i: (e, 0, i)),
            pl.BlockSpec((1, slots, cols), lambda e, i: (e, 0, 0)),
        ],
        out_specs=pl.BlockSpec((1, tile, cols), lambda e, i: (e, i, 0)),
        compiler_params=params(),
        cost_estimate=cost(2 * a.size * cols, 2 * (a.size + b.size + experts * m * cols)),
    )(a, b)


def gather_blocks(mine, n, exp_count):
    others = jnp.stack([lax.ppermute(mine, "ctx", shift(n, s)) for s in range(1, n)])
    slabs = []
    for dx in range(exp_count):
        part = others if dx == 0 else lax.ppermute(others, "exp", shift(exp_count, dx))
        slabs += [part, lax.ppermute(part, "tp", shift(2, 1))]
    return slabs


def per_device(tokens, out_grad, expert_ids, gate_weights, gate_matrix, up_matrix, down_matrix):
    n = lax.axis_size("ctx")
    exp_count = lax.axis_size("exp")
    x = lax.axis_index("exp")
    c = lax.axis_index("tp")
    local_count, depth, hidden_units = gate_matrix.shape
    experts = local_count * exp_count
    block, _ = tokens.shape
    width = depth // (exp_count * 2)
    slots = n * CAP
    here = jnp.stack([x, c]).astype(jnp.int32)
    column = (x * 2 + c) * width

    names = jnp.arange(experts, dtype=jnp.int32)[:, None]
    chosen = [expert_ids[:, k][None, :] == names for k in range(expert_ids.shape[1])]
    member = functools.reduce(jnp.logical_or, chosen)
    before = jnp.arange(block)[:, None] <= jnp.arange(block)[None, :]
    order = jnp.dot(member.astype(BF16), before.astype(BF16), preferred_element_type=F32)
    slot = jnp.where(member, order - 1.0, -1.0)
    weight = sum(jnp.where(ch, gate_weights[:, k][None, :], 0.0) for k, ch in enumerate(chosen))
    meta = jnp.concatenate([slot, weight], axis=0)

    token_part = lax.dynamic_slice_in_dim(tokens, column, width, axis=1)
    grad_part = lax.dynamic_slice_in_dim(out_grad, column, width, axis=1)
    token_slabs = gather_blocks(token_part, n, exp_count)
    metas = [meta] + [lax.ppermute(meta, "ctx", shift(n, s)) for s in range(1, n)]
    grad_slabs = gather_blocks(grad_part, n, exp_count)

    slab_specs = [whole((block, depth))] + [whole((n - 1, block, width))] * (2 * exp_count)
    meta_specs = [whole(meta.shape)] * n
    tile = min(256, hidden_units)
    grid = (local_count, hidden_units // tile)
    packed = jax.ShapeDtypeStruct((local_count, slots, depth), BF16)
    packed_spec = pl.BlockSpec((local_count, slots, depth), lambda *_: (0, 0, 0))
    units = lambda dtype: jax.ShapeDtypeStruct((local_count, slots, hidden_units), dtype)
    units_spec = pl.BlockSpec((1, slots, tile), lambda e, j, *_: (e, 0, j))
    flops = 2 * local_count * slots * depth * hidden_units
    weight_bytes = 2 * gate_matrix.size

    xp, hidden, act, dact = pl.pallas_call(
        functools.partial(forward_kernel, n, exp_count, width),
        out_shape=(packed, units(BF16), units(F32), units(F32)),
        grid_spec=pltpu.PrefetchScalarGridSpec(
            num_scalar_prefetch=1,
            grid=grid,
            in_specs=slab_specs + meta_specs
            + [pl.BlockSpec((1, depth, tile), lambda e, j, *_: (e, 0, j))] * 2,
            out_specs=(packed_spec, units_spec, units_spec, units_spec),
        ),
        compiler_params=params(),
        cost_estimate=cost(2 * flops, 2 * weight_bytes),
    )(here, tokens, *token_slabs, *metas, gate_matrix, up_matrix)

    gp, gate_grad, up_grad = pl.pallas_call(
        functools.partial(hidden_kernel, n, exp_count, width, experts),
        out_shape=(packed, units(BF16), units(BF16)),
        grid_spec=pltpu.PrefetchScalarGridSpec(
            num_scalar_prefetch=1,
            grid=grid,
            in_specs=slab_specs + meta_specs
            + [pl.BlockSpec((1, tile, depth), lambda e, j, *_: (e, j, 0)), units_spec, units_spec],
            out_specs=(packed_spec, units_spec, units_spec),
        ),
        compiler_params=params(),
        cost_estimate=cost(flops, weight_bytes),
    )(here, out_grad, *grad_slabs, *metas, down_matrix, act, dact)

    def row_grads(slab, add):
        part_spec = pl.BlockSpec((local_count, width, hidden_units), lambda i, pick, *_: (0, pick[0], 0))
        adds = [] if add is None else [add]
        return pl.pallas_call(
            functools.partial(rows_kernel, n, local_count, add is not None),
            out_shape=jax.ShapeDtypeStruct((n, block, width), BF16),
            grid_spec=pltpu.PrefetchScalarGridSpec(
                num_scalar_prefetch=2,
                grid=(1,),
                in_specs=meta_specs
                + [whole((local_count, slots, hidden_units))] * 2
                + [part_spec] * 2
                + [whole((n, block, width))] * len(adds),
                out_specs=whole((n, block, width)),
            ),
            compiler_params=params(),
            cost_estimate=cost(2 * flops * width // depth, 2 * weight_bytes * width // depth),
        )(slab.reshape(1).astype(jnp.int32), here, *metas, gate_grad, up_grad, gate_matrix, up_matrix, *adds)

    def slab_of(dx, dc):
        return lax.rem(x + dx, exp_count) * 2 + lax.rem(c + dc, 2)

    order_dx = list(range(1, exp_count)) + [0]
    siblings = [lax.ppermute(row_grads(slab_of(dx, 1), None), "tp", shift(2, 1)) for dx in order_dx]
    received = []
    for dx, sibling in zip(order_dx, siblings):
        own = row_grads(slab_of(dx, 0), sibling)
        if dx:
            received.append(lax.ppermute(own, "exp", shift(exp_count, dx)))
    total = own.astype(F32)
    for part in received:
        total = total + part.astype(F32)
    rounded = total.astype(BF16)
    final = total[0]
    for s in range(1, n):
        final = final + lax.ppermute(rounded[s], "ctx", shift(n, -s)).astype(F32)
    grad_tokens = final.astype(BF16)

    grad_down = weight_grad(hidden, gp)
    grad_gate = weight_grad(xp, gate_grad)
    grad_up = weight_grad(xp, up_grad)
    return (grad_gate, grad_up, grad_down, grad_tokens)


def solution(mesh):
    in_specs = (
        P(("groups", "ctx"), None),
        P(("groups", "ctx"), None),
        P(("groups", "ctx"), None),
        P(("groups", "ctx"), None),
        P("exp", None, ("ctx", "tp")),
        P("exp", None, ("ctx", "tp")),
        P("exp", ("ctx", "tp"), None),
    )
    out_specs = (
        P(("groups", "exp"), None, ("ctx", "tp")),
        P(("groups", "exp"), None, ("ctx", "tp")),
        P(("groups", "exp"), ("ctx", "tp"), None),
        P(("groups", "ctx"), ("exp", "tp")),
    )
    return jax.shard_map(
        per_device, mesh=mesh, in_specs=in_specs, out_specs=out_specs, check_vma=False
    )
```

```python
import functools

import jax
import jax.numpy as jnp
from jax import lax
from jax.experimental import pallas as pl
from jax.experimental.pallas import tpu as pltpu
from jax.sharding import PartitionSpec as P

CAP = 72
VM = pltpu.VMEM
F32 = jnp.float32
BF16 = jnp.bfloat16
NN = (((1,), (0,)), ((), ()))
NT = (((1,), (1,)), ((), ()))
TN = (((0,), (0,)), ((), ()))


def mm(a, b, dims):
    return lax.dot_general(a, b, dims, preferred_element_type=F32)


def params(mib):
    return pltpu.CompilerParams(vmem_limit_bytes=mib * 1024 * 1024)


def cost(flops, nbytes):
    return pl.CostEstimate(flops=int(flops), bytes_accessed=int(nbytes), transcendentals=0)


def vmem(count):
    return [pl.BlockSpec(memory_space=VM)] * count


def far(array):
    return pltpu.with_memory_space_constraint(array, pltpu.HBM)


def anywhere(count):
    return [pl.BlockSpec(memory_space=pl.ANY)] * count


def hbm(count):
    return [pl.BlockSpec(memory_space=pltpu.HBM)] * count


SCALARS = pl.BlockSpec(memory_space=pltpu.SMEM)


def shift(count, by):
    return [(i, (i + by) % count) for i in range(count)]


def pair_rows(metas, row, pair):
    first = metas[2 * pair][pl.ds(row, 1), :]
    second = metas[2 * pair + 1][pl.ds(row, 1), :]
    return first, second


def pair_one_hot(metas, expert, pair):
    first, second = pair_rows(metas, expert, pair)
    second = jnp.where(second >= 0, second + CAP, second)
    slot = jnp.concatenate([first, second], axis=1)
    rows = lax.broadcasted_iota(jnp.int32, (2 * CAP, slot.shape[1]), 0).astype(F32)
    return rows == slot


class Gathered:
    def __init__(self, refs, pieces):
        self.own = refs[0]
        self.pieces = list(zip(pieces, refs[1:]))

    def pack(self, here, exp_count, slab, pair, hot, scale, store):
        for (dx, dc, offset), ref in self.pieces:
            x = lax.rem(here[0] + exp_count - dx, exp_count)
            c = lax.rem(here[1] + dc, 2)
            width = ref.shape[2]
            column = pl.multiple_of((x * 2 + c) * slab + offset, 128)
            if pair == 0:
                rows = jnp.concatenate([self.own[:, pl.ds(column, width)], ref[0]], axis=0)
            else:
                rows = jnp.concatenate([ref[2 * pair - 1], ref[2 * pair]], axis=0)
            packed = mm(hot, rows, NN)
            if scale is not None:
                packed = packed * scale
            store(column, width, packed.astype(BF16))


def start_all(copies):
    for copy in copies:
        copy.start()


def wait_all(copies):
    for copy in copies:
        copy.wait()


class Saves:
    def __init__(self, sems):
        self.sems, self.copies = sems, []

    def __call__(self, src, dst):
        copy = pltpu.make_async_copy(src, dst, self.sems.at[len(self.copies)])
        copy.start()
        self.copies.append(copy)


def load_all(srcs, dsts, sems):
    return [pltpu.make_async_copy(src, dst, sems.at[k]) for k, (src, dst) in enumerate(zip(srcs, dsts))]


def forward_kernel(n, exp_count, pieces, slab, tile, local, here_ref, *refs):
    metas, refs = refs[:n], refs[n:]
    loads, refs = refs[:1 + len(pieces)], refs[1 + len(pieces):]
    gate_hbm, up_hbm, xp_out, hid_out, act_out, dact_out = refs[:6]
    staged, refs = refs[6:6 + len(loads)], refs[6 + len(loads):]
    xp_ref, hid_ref, act_ref, dact_ref, gate_w, up_w, load_sems, sems, save_sems = refs
    data = Gathered(staged, pieces)
    steps = gate_hbm.shape[2] // tile
    ring = gate_w.shape[0]
    expert = here_ref[0] * gate_hbm.shape[0] + local

    def fetch(j):
        units = pl.ds(j * tile, tile)
        return [
            pltpu.make_async_copy(src.at[local, :, units], dst.at[j % ring], sems.at[k, j % ring])
            for k, (src, dst) in enumerate(((gate_hbm, gate_w), (up_hbm, up_w)))
        ]

    first = load_all(loads, staged, load_sems)
    save = Saves(save_sems)
    start_all(first)
    start_all(fetch(0))
    wait_all(first)
    for j in range(1, min(ring, steps)):
        start_all(fetch(j))
    for pair in range(n // 2):
        hot = pair_one_hot(metas, expert, pair).astype(BF16)

        def store(column, width, value):
            xp_ref[pl.ds(pair * 2 * CAP, 2 * CAP), pl.ds(column, width)] = value

        data.pack(here_ref, exp_count, slab, pair, hot, None, store)
    save(xp_ref, xp_out)
    for j in range(steps):
        wait_all(fetch(j))
        units = pl.ds(j * tile, tile)
        rows = xp_ref[...]
        gate = mm(rows, gate_w[j % ring], NN)
        up = mm(rows, up_w[j % ring], NN)
        if j + ring < steps:
            start_all(fetch(j + ring))
        sig = jax.nn.sigmoid(gate)
        act = gate * sig
        hid_ref[:, units] = (act * up).astype(BF16)
        act_ref[:, units] = act
        dact_ref[:, units] = up * sig * (1.0 + gate * (1.0 - sig))
        save(act_ref.at[:, units], act_out.at[:, units])
        save(dact_ref.at[:, units], dact_out.at[:, units])
    save(hid_ref, hid_out)
    wait_all(save.copies)


def slab_chunks(here_ref, gate_hbm, up_hbm, gate_w, up_w, sems, slabs):
    ring, width, _ = gate_w.shape
    chunks = []
    for s in range(slabs):
        rows = pl.ds(pl.multiple_of(here_ref[2 + s] * width, 128), width)
        for e in range(gate_hbm.shape[0]):
            k = len(chunks) % ring
            chunks.append([
                pltpu.make_async_copy(src.at[e, rows, :], dst.at[k], sems.at[m, k])
                for m, (src, dst) in enumerate(((gate_hbm, gate_w), (up_hbm, up_w)))
            ])
    return chunks


def slab_rows(n, here_ref, metas, gg_ref, ug_ref, gate_w, up_w, stream, used, out_ref, save):
    local_count = gg_ref.shape[0]
    ring = gate_w.shape[0]
    begun = used
    for s in range(out_ref.shape[0]):
        terms = []
        for local in range(local_count):
            wait_all(stream[used])
            k = (used - begun) % ring
            term = mm(gg_ref[local], gate_w[k], NT) + mm(ug_ref[local], up_w[k], NT)
            terms.append(term.astype(BF16))
            if used + ring < len(stream):
                start_all(stream[used + ring])
            used += 1
        for pair in range(n // 2):
            total = None
            for local, term in enumerate(terms):
                expert = here_ref[0] * local_count + local
                hot = pair_one_hot(metas, expert, pair).astype(BF16)
                part = mm(hot, term[pair * 2 * CAP:(pair + 1) * 2 * CAP], TN)
                total = part if total is None else total + part
            half = total.shape[0] // 2
            for j in range(2):
                out_ref[s, (2 * pair + j - 1) % n] = total[j * half:(j + 1) * half].astype(BF16)
        save(out_ref.at[s], s)


def backward_kernel(n, exp_count, pieces, slab, tile, local_count, slabs, here_ref, *refs):
    metas, refs = refs[:n], refs[n:]
    loads, refs = refs[:1 + len(pieces)], refs[1 + len(pieces):]
    act_hbm, refs = refs[:2 * local_count], refs[2 * local_count:]
    gate_hbm, up_hbm, down_hbm, gp_hbm, gg_hbm, ug_hbm, gg_ref, ug_ref = refs[:8]
    outs, refs = refs[8:8 + slabs], refs[8 + slabs:]
    staged, refs = refs[:len(loads)], refs[len(loads):]
    (act_ref, dact_ref, gp_ref, out_ref, gate_w, up_w, down_w,
     load_sems, act_sems, slab_sems, down_sems, save_sems) = refs
    data = Gathered(staged, pieces)
    steps = gg_ref.shape[2] // tile
    ring = gate_w.shape[0]

    first = load_all(loads, staged, load_sems)
    scales = []
    for e in range(local_count):
        scales.append([
            pltpu.make_async_copy(act_hbm[e], act_ref.at[e], act_sems.at[0, e]),
            pltpu.make_async_copy(act_hbm[local_count + e], dact_ref.at[e], act_sems.at[1, e]),
        ])
    downs = []
    for e in range(local_count):
        for j in range(steps):
            k = len(downs) % ring
            src = down_hbm.at[e, pl.ds(j * tile, tile), :]
            downs.append([pltpu.make_async_copy(src, down_w.at[k], down_sems.at[k])])
    stream = downs + slab_chunks(here_ref, gate_hbm, up_hbm, gate_w, up_w, slab_sems, slabs)
    save = Saves(save_sems)

    start_all(first)
    start_all(stream[0])
    wait_all(first)
    start_all(scales[0])
    for copies in stream[1:ring]:
        start_all(copies)
    for copies in scales[1:]:
        start_all(copies)
    experts = local_count * exp_count
    used = 0
    for local in range(local_count):
        expert = here_ref[0] * local_count + local
        for pair in range(n // 2):
            hot = pair_one_hot(metas, expert, pair)
            weights = jnp.concatenate(pair_rows(metas, experts + expert, pair), axis=1)
            scale = jnp.sum(jnp.where(hot, weights, 0.0), axis=1, keepdims=True)

            def store(column, width, value):
                gp_ref[local, pl.ds(pair * 2 * CAP, 2 * CAP), pl.ds(column, width)] = value

            data.pack(here_ref, exp_count, slab, pair, hot.astype(BF16), scale, store)
        save(gp_ref.at[local], gp_hbm.at[local])
        wait_all(scales[local])
        for j in range(steps):
            wait_all(stream[used])
            units = pl.ds(j * tile, tile)
            hidden_grad = mm(gp_ref[local], down_w[used % ring], NT)
            ug_ref[local, :, units] = (hidden_grad * act_ref[local, :, units]).astype(BF16)
            gg_ref[local, :, units] = (hidden_grad * dact_ref[local, :, units]).astype(BF16)
            if used + ring < len(stream):
                start_all(stream[used + ring])
            used += 1
        save(gg_ref.at[local], gg_hbm.at[local])
        save(ug_ref.at[local], ug_hbm.at[local])
    slab_rows(n, here_ref, metas, gg_ref, ug_ref, gate_w, up_w, stream, used, out_ref,
              lambda src, s: save(src, outs[s]))
    wait_all(save.copies)


def home_kernel(n, slabs, here_ref, *refs):
    metas, refs = refs[:n], refs[n:]
    gg_ref, ug_ref, gate_hbm, up_hbm = refs[:4]
    outs = refs[4:4 + slabs]
    out_ref, gate_w, up_w, slab_sems, save_sems = refs[4 + slabs:]
    stream = slab_chunks(here_ref, gate_hbm, up_hbm, gate_w, up_w, slab_sems, slabs)
    save = Saves(save_sems)
    for copies in stream[:gate_w.shape[0]]:
        start_all(copies)
    slab_rows(n, here_ref, metas, gg_ref, ug_ref, gate_w, up_w, stream, 0, out_ref,
              lambda src, s: save(src, outs[s]))
    wait_all(save.copies)


def hold_kernel(*refs):
    del refs


def hold(arrays, after):
    return pl.pallas_call(
        hold_kernel,
        out_shape=[jax.ShapeDtypeStruct(a.shape, a.dtype) for a in arrays],
        in_specs=anywhere(len(arrays) + len(after)),
        out_specs=anywhere(len(arrays)),
        input_output_aliases={k: k for k in range(len(arrays))},
        compiler_params=params(4),
        cost_estimate=cost(0, 0),
    )(*arrays, *after)


def weights_kernel(counts, xp_ref, hid_ref, gg_ref, ug_ref, gp_ref, *refs):
    gate_out, up_out, down_out = refs[-3:]
    step = pl.program_id(0)
    tile = gate_out.shape[1]

    def columns(at):
        return pl.ds(pl.multiple_of(at * tile, 128), tile)

    @pl.when(step < counts)
    def _():
        gate_out[0] = mm(xp_ref[:, columns(step)], gg_ref[0], TN).astype(BF16)

    @pl.when(jnp.logical_and(step >= counts, step < 2 * counts))
    def _():
        up_out[0] = mm(xp_ref[:, columns(step - counts)], ug_ref[0], TN).astype(BF16)

    @pl.when(step >= 2 * counts)
    def _():
        down_out[0] = mm(hid_ref[...], gp_ref[0, :, columns(step - 2 * counts)], TN).astype(BF16)


def weight_grads(local, xp, hidden, gate_grad, up_grad, gp, before):
    slots, depth = xp.shape
    local_count, _, hidden_units = gate_grad.shape
    tile = 1024
    counts = depth // tile
    shapes = [(local_count, depth, hidden_units)] * 2 + [(local_count, hidden_units, depth)]

    def place(which, step):
        return jnp.clip(step - which * counts, 0, counts - 1)

    one = lambda array: pl.BlockSpec((1, *array.shape[1:]), lambda i: (local, 0, 0))
    all_of = lambda array: pl.BlockSpec(array.shape, lambda i: (0, 0))
    return pl.pallas_call(
        functools.partial(weights_kernel, counts),
        out_shape=[jax.ShapeDtypeStruct(shape, BF16) for shape in shapes],
        grid=(3 * counts,),
        in_specs=[all_of(xp), all_of(hidden), one(gate_grad), one(up_grad), one(gp)]
        + anywhere(len(before)),
        out_specs=[
            pl.BlockSpec((1, tile, hidden_units), lambda i: (local, place(0, i), 0)),
            pl.BlockSpec((1, tile, hidden_units), lambda i: (local, place(1, i), 0)),
            pl.BlockSpec((1, hidden_units, tile), lambda i: (local, 0, place(2, i))),
        ],
        input_output_aliases={5 + k: k for k in range(len(before))},
        compiler_params=params(40),
        cost_estimate=cost(6 * slots * depth * hidden_units, 6 * depth * hidden_units),
    )(far(xp), far(hidden), far(gate_grad), far(up_grad), far(gp), *before)


def gather_ctx(mine, n):
    return [lax.ppermute(mine, "ctx", shift(n, s)) for s in range(1, n)]


def exchange(received, exp_count):
    others = jnp.stack(received)
    return others, [lax.ppermute(others, "exp", shift(exp_count, dx)) for dx in range(1, exp_count)]


def siblings(parts, offset):
    pieces, arrays = [], []
    for dx, part in enumerate(parts):
        pieces += [(dx, 0, offset), (dx, 1, offset)]
        arrays += [part, lax.ppermute(part, "tp", shift(2, 1))]
    return pieces, arrays


def per_device(tokens, out_grad, expert_ids, gate_weights, gate_matrix, up_matrix, down_matrix):
    n = lax.axis_size("ctx")
    exp_count = lax.axis_size("exp")
    x = lax.axis_index("exp")
    c = lax.axis_index("tp")
    local_count, depth, hidden_units = gate_matrix.shape
    experts = local_count * exp_count
    block, _ = tokens.shape
    width = depth // (exp_count * 2)
    slots = n * CAP
    here = jnp.stack([x, c, (x * 2 + c) * width, 0]).astype(jnp.int32)

    names = jnp.arange(experts, dtype=jnp.int32)[:, None]
    chosen = [expert_ids[:, k][None, :] == names for k in range(expert_ids.shape[1])]
    member = functools.reduce(jnp.logical_or, chosen)
    before = jnp.arange(block)[:, None] <= jnp.arange(block)[None, :]
    order = jnp.dot(member.astype(BF16), before.astype(BF16), preferred_element_type=F32)
    slot = jnp.where(member, order - 1.0, -1.0)
    weight = sum(jnp.where(ch, gate_weights[:, k][None, :], 0.0) for k, ch in enumerate(chosen))
    meta = jnp.concatenate([slot, weight], axis=0)

    half = width // 256 * 128
    cuts = [(0, half), (half, width - half)]

    def mine(array, piece):
        offset, size = cuts[piece]
        return lax.dynamic_slice_in_dim(array, (x * 2 + c) * width + offset, size, axis=1)

    m = n - 1
    step = hold(gather_ctx(mine(tokens, 0), n) + gather_ctx(meta, n), [])
    t0, metas = step[:m], [meta, *step[m:]]
    t0, t0_exp = exchange(t0, exp_count)
    step = hold(gather_ctx(mine(tokens, 1), n) + t0_exp, [])
    t1, t0_exp = step[:m], step[m:]
    t1, t1_exp = exchange(t1, exp_count)
    t_pieces, t_arrays = siblings([t0, *t0_exp], 0)
    step = hold(gather_ctx(mine(out_grad, 0), n) + t1_exp, t_arrays)
    g0, t1_exp = step[:m], step[m:]
    g0, g0_exp = exchange(g0, exp_count)
    more_pieces, more_arrays = siblings([t1, *t1_exp], half)
    t_pieces += more_pieces
    t_arrays += more_arrays
    g1 = gather_ctx(mine(out_grad, 1), n)

    tile = min(512, hidden_units)
    fine = min(256, hidden_units)
    flops = 2 * local_count * slots * depth * hidden_units
    dma = pltpu.SemaphoreType.DMA
    stack = lambda cols, dtype: pltpu.HBM((slots, cols), dtype)
    near = lambda shape: pltpu.HBM(shape, BF16)
    loads = [tokens, *t_arrays]
    forward = []
    for local in range(local_count):
        forward.append(pl.pallas_call(
            functools.partial(forward_kernel, n, exp_count, t_pieces, width, fine, local),
            out_shape=(stack(depth, BF16), stack(hidden_units, BF16),
                       stack(hidden_units, F32), stack(hidden_units, F32)),
            in_specs=[SCALARS] + vmem(n) + anywhere(len(loads)) + hbm(2),
            out_specs=hbm(4),
            scratch_shapes=[VM(a.shape, BF16) for a in loads]
            + [VM((slots, depth), BF16), VM((slots, hidden_units), BF16)]
            + [VM((slots, hidden_units), F32)] * 2 + [VM((2, depth, fine), BF16)] * 2
            + [dma((len(loads),)), dma((2, 2)), dma((2 + 2 * (hidden_units // fine),))],
            compiler_params=params(34),
            cost_estimate=cost(2 * flops // local_count, 0),
        )(here, *metas, *loads, far(gate_matrix), far(up_matrix)))
        if local == 0:
            step = hold(g1 + g0_exp, forward[0][2:3])
            g1, g0_exp = step[:m], step[m:]
            g1, g1_exp = exchange(g1, exp_count)
    xps, hiddens, acts, dacts = zip(*forward)
    g1_exp = hold(g1_exp, acts[1:])
    g_pieces, g_arrays = siblings([g0, *g0_exp], 0)
    more_pieces, more_arrays = siblings([g1, *g1_exp], half)
    g_pieces += more_pieces
    g_arrays += more_arrays

    away = [(dx, dc) for dx in range(1, exp_count) for dc in (1, 0)]
    home = [(0, 1), (0, 0)]

    def where(slabs):
        at = [lax.rem(x + dx, exp_count) * 2 + lax.rem(c + dc, 2) for dx, dc in slabs]
        return jnp.stack([x, c, *at]).astype(jnp.int32)

    part = (n, block, width)
    units = (local_count, slots, hidden_units)
    ring = 3
    slab_buffers = [VM((ring, width, hidden_units), BF16)] * 2
    loads = [out_grad, *g_arrays]
    gp, gate_grad, up_grad, gate_near, up_near, *away_outs = pl.pallas_call(
        functools.partial(
            backward_kernel, n, exp_count, g_pieces, width, tile, local_count, len(away)
        ),
        out_shape=[near((local_count, slots, depth)), near(units), near(units)]
        + [VM(units, BF16)] * 2 + [near(part)] * len(away),
        in_specs=[SCALARS] + vmem(n) + anywhere(len(loads)) + hbm(2 * local_count + 3),
        out_specs=hbm(3) + vmem(2) + hbm(len(away)),
        scratch_shapes=[VM(a.shape, BF16) for a in loads]
        + [VM(units, F32)] * 2 + [VM((local_count, slots, depth), BF16)]
        + [VM((len(away), *part), BF16)] + slab_buffers
        + [VM((ring, tile, depth), BF16), dma((len(loads),)), dma((2, local_count)),
           dma((2, ring)), dma((ring,)), dma((3 * local_count + len(away),))],
        compiler_params=params(48),
        cost_estimate=cost(2 * flops, 0),
    )(
        where(away), *metas, *loads, *map(far, acts), *map(far, dacts),
        far(gate_matrix), far(up_matrix), far(down_matrix),
    )
    away_outs = dict(zip(away, away_outs))
    early = n // 2

    def chip_sum(outs, dx, rows, sibling):
        return outs[dx, 0][rows].astype(F32) + sibling[rows].astype(F32)

    parts = [slice(0, early), slice(early, n)]
    arrived = [[], []]
    for dx in range(1, exp_count):
        sibling = lax.ppermute(away_outs[dx, 1], "tp", shift(2, 1))
        for k, rows in enumerate(parts):
            out = chip_sum(away_outs, dx, rows, sibling).astype(BF16)
            arrived[k].append(lax.ppermute(out, "exp", shift(exp_count, dx)))

    home_outs = pl.pallas_call(
        functools.partial(home_kernel, n, len(home)),
        out_shape=[near(part)] * len(home),
        in_specs=[SCALARS] + vmem(n + 2) + hbm(2),
        out_specs=hbm(len(home)),
        scratch_shapes=[VM((len(home), *part), BF16)] + slab_buffers
        + [dma((2, ring)), dma((len(home),))],
        compiler_params=params(22),
        cost_estimate=cost(4 * flops * width // depth, 0),
    )(where(home), *metas, gate_near, up_near, far(gate_matrix), far(up_matrix))
    home_outs = dict(zip(home, home_outs))
    sibling = lax.ppermute(home_outs[0, 1], "tp", shift(2, 1))
    final = None
    for k, rows in enumerate(parts):
        total = chip_sum(home_outs, 0, rows, sibling)
        for other in arrived[k]:
            total = total + other.astype(F32)
        rounded = total.astype(BF16)
        for j in range(total.shape[0]):
            s = rows.start + j + 1
            if s < n:
                term = lax.ppermute(rounded[j], "ctx", shift(n, -s)).astype(F32)
            else:
                term = total[j]
            final = term if final is None else final + term
    grad_tokens = final.astype(BF16)

    grads = []
    for local in range(local_count):
        grads = weight_grads(
            local, xps[local], hiddens[local], gate_grad, up_grad, gp, grads
        )
    grad_gate, grad_up, grad_down = grads
    return (grad_gate, grad_up, grad_down, grad_tokens)


def solution(mesh):
    in_specs = (
        P(("groups", "ctx"), None),
        P(("groups", "ctx"), None),
        P(("groups", "ctx"), None),
        P(("groups", "ctx"), None),
        P("exp", None, ("ctx", "tp")),
        P("exp", None, ("ctx", "tp")),
        P("exp", ("ctx", "tp"), None),
    )
    out_specs = (
        P(("groups", "exp"), None, ("ctx", "tp")),
        P(("groups", "exp"), None, ("ctx", "tp")),
        P(("groups", "exp"), ("ctx", "tp"), None),
        P(("groups", "ctx"), ("exp", "tp")),
    )
    return jax.shard_map(
        per_device, mesh=mesh, in_specs=in_specs, out_specs=out_specs, check_vma=False
    )
```

```python
import functools

import jax
import jax.numpy as jnp
from jax import lax
from jax.experimental import pallas as pl
from jax.experimental.pallas import tpu as pltpu
from jax.sharding import PartitionSpec as P

CAP = 72
VM = pltpu.VMEM
F32 = jnp.float32
BF16 = jnp.bfloat16
NN = (((1,), (0,)), ((), ()))
NT = (((1,), (1,)), ((), ()))
TN = (((0,), (0,)), ((), ()))


def mm(a, b, dims):
    return lax.dot_general(a, b, dims, preferred_element_type=F32)


def params(mib):
    return pltpu.CompilerParams(vmem_limit_bytes=mib * 1024 * 1024)


def cost(flops, nbytes):
    return pl.CostEstimate(flops=int(flops), bytes_accessed=int(nbytes), transcendentals=0)


def vmem(count):
    return [pl.BlockSpec(memory_space=VM)] * count


def far(array):
    return pltpu.with_memory_space_constraint(array, pltpu.HBM)


def anywhere(count):
    return [pl.BlockSpec(memory_space=pl.ANY)] * count


def hbm(count):
    return [pl.BlockSpec(memory_space=pltpu.HBM)] * count


SCALARS = pl.BlockSpec(memory_space=pltpu.SMEM)


def shift(count, by):
    return [(i, (i + by) % count) for i in range(count)]


def pair_rows(metas, row, pair):
    first = metas[2 * pair][pl.ds(row, 1), :]
    second = metas[2 * pair + 1][pl.ds(row, 1), :]
    return first, second


def pair_one_hot(metas, expert, pair):
    first, second = pair_rows(metas, expert, pair)
    second = jnp.where(second >= 0, second + CAP, second)
    slot = jnp.concatenate([first, second], axis=1)
    rows = lax.broadcasted_iota(jnp.int32, (2 * CAP, slot.shape[1]), 0).astype(F32)
    return rows == slot


class Gathered:
    def __init__(self, refs, pieces):
        self.own = refs[0]
        self.pieces = list(zip(pieces, refs[1:]))

    def pack(self, here, exp_count, slab, pair, hot, scale, store):
        for (dx, dc, offset), ref in self.pieces:
            x = lax.rem(here[0] + exp_count - dx, exp_count)
            c = lax.rem(here[1] + dc, 2)
            width = ref.shape[2]
            column = pl.multiple_of((x * 2 + c) * slab + offset, 128)
            if pair == 0:
                rows = jnp.concatenate([self.own[:, pl.ds(column, width)], ref[0]], axis=0)
            else:
                rows = jnp.concatenate([ref[2 * pair - 1], ref[2 * pair]], axis=0)
            packed = mm(hot, rows, NN)
            if scale is not None:
                packed = packed * scale
            store(column, width, packed.astype(BF16))


def start_all(copies):
    for copy in copies:
        copy.start()


def wait_all(copies):
    for copy in copies:
        copy.wait()


class Saves:
    def __init__(self, sems):
        self.sems, self.copies = sems, []

    def __call__(self, src, dst):
        copy = pltpu.make_async_copy(src, dst, self.sems.at[len(self.copies)])
        copy.start()
        self.copies.append(copy)


def load_all(srcs, dsts, sems):
    return [pltpu.make_async_copy(src, dst, sems.at[k]) for k, (src, dst) in enumerate(zip(srcs, dsts))]


def forward_kernel(n, exp_count, pieces, slab, tile, local, here_ref, *refs):
    metas, refs = refs[:n], refs[n:]
    loads, refs = refs[:1 + len(pieces)], refs[1 + len(pieces):]
    gate_hbm, up_hbm, xp_out, hid_out, act_out, dact_out, token_ref = refs[:7]
    staged, refs = refs[7:7 + len(loads)], refs[7 + len(loads):]
    token_ref[...] = jnp.zeros_like(token_ref)
    xp_ref, hid_ref, act_ref, dact_ref, gate_w, up_w, load_sems, sems, save_sems = refs
    data = Gathered(staged, pieces)
    steps = gate_hbm.shape[2] // tile
    ring = gate_w.shape[0]
    expert = here_ref[0] * gate_hbm.shape[0] + local

    def fetch(j):
        units = pl.ds(j * tile, tile)
        return [
            pltpu.make_async_copy(src.at[local, :, units], dst.at[j % ring], sems.at[k, j % ring])
            for k, (src, dst) in enumerate(((gate_hbm, gate_w), (up_hbm, up_w)))
        ]

    first = load_all(loads, staged, load_sems)
    save = Saves(save_sems)
    start_all(first)
    start_all(fetch(0))
    wait_all(first)
    for j in range(1, min(ring, steps)):
        start_all(fetch(j))
    for pair in range(n // 2):
        hot = pair_one_hot(metas, expert, pair).astype(BF16)

        def store(column, width, value):
            xp_ref[pl.ds(pair * 2 * CAP, 2 * CAP), pl.ds(column, width)] = value

        data.pack(here_ref, exp_count, slab, pair, hot, None, store)
    save(xp_ref, xp_out)
    for j in range(steps):
        wait_all(fetch(j))
        units = pl.ds(j * tile, tile)
        rows = xp_ref[...]
        gate = mm(rows, gate_w[j % ring], NN)
        up = mm(rows, up_w[j % ring], NN)
        if j + ring < steps:
            start_all(fetch(j + ring))
        sig = jax.nn.sigmoid(gate)
        act = gate * sig
        hid_ref[:, units] = (act * up).astype(BF16)
        act_ref[:, units] = act
        dact_ref[:, units] = up * sig * (1.0 + gate * (1.0 - sig))
        save(act_ref.at[:, units], act_out.at[:, units])
        save(dact_ref.at[:, units], dact_out.at[:, units])
    save(hid_ref, hid_out)
    wait_all(save.copies)


def slab_chunks(here_ref, gate_hbm, up_hbm, gate_w, up_w, sems, slabs):
    ring, width, _ = gate_w.shape
    chunks = []
    for s in range(slabs):
        rows = pl.ds(pl.multiple_of(here_ref[2 + s] * width, 128), width)
        for e in range(gate_hbm.shape[0]):
            k = len(chunks) % ring
            chunks.append([
                pltpu.make_async_copy(src.at[e, rows, :], dst.at[k], sems.at[m, k])
                for m, (src, dst) in enumerate(((gate_hbm, gate_w), (up_hbm, up_w)))
            ])
    return chunks


def slab_rows(n, here_ref, metas, gg_ref, ug_ref, gate_w, up_w, stream, used, out_ref, save):
    local_count = gg_ref.shape[0]
    ring = gate_w.shape[0]
    begun = used
    for s in range(out_ref.shape[0]):
        terms = []
        for local in range(local_count):
            wait_all(stream[used])
            k = (used - begun) % ring
            term = mm(gg_ref[local], gate_w[k], NT) + mm(ug_ref[local], up_w[k], NT)
            terms.append(term.astype(BF16))
            if used + ring < len(stream):
                start_all(stream[used + ring])
            used += 1
        for pair in range(n // 2):
            total = None
            for local, term in enumerate(terms):
                expert = here_ref[0] * local_count + local
                hot = pair_one_hot(metas, expert, pair).astype(BF16)
                part = mm(hot, term[pair * 2 * CAP:(pair + 1) * 2 * CAP], TN)
                total = part if total is None else total + part
            half = total.shape[0] // 2
            for j in range(2):
                out_ref[s, (2 * pair + j - 1) % n] = total[j * half:(j + 1) * half].astype(BF16)
        save(out_ref.at[s], s)


def backward_kernel(n, exp_count, pieces, slab, tile, local_count, slabs, here_ref, *refs):
    metas, refs = refs[:n], refs[n:]
    loads, refs = refs[:1 + len(pieces)], refs[1 + len(pieces):]
    act_hbm, refs = refs[:2 * local_count], refs[2 * local_count:]
    gate_hbm, up_hbm, down_hbm, gp_hbm, gg_hbm, ug_hbm = refs[:6]
    outs, refs = refs[6:6 + slabs], refs[6 + slabs:]
    staged, refs = refs[:len(loads)], refs[len(loads):]
    (act_ref, dact_ref, gp_ref, gg_ref, ug_ref, out_ref, gate_w, up_w, down_w,
     load_sems, act_sems, slab_sems, down_sems, save_sems) = refs
    data = Gathered(staged, pieces)
    steps = gg_ref.shape[2] // tile
    ring = gate_w.shape[0]

    first = load_all(loads, staged, load_sems)
    scales = []
    for e in range(local_count):
        scales.append([
            pltpu.make_async_copy(act_hbm[e], act_ref.at[e], act_sems.at[0, e]),
            pltpu.make_async_copy(act_hbm[local_count + e], dact_ref.at[e], act_sems.at[1, e]),
        ])
    downs = []
    for e in range(local_count):
        for j in range(steps):
            k = len(downs) % ring
            src = down_hbm.at[e, pl.ds(j * tile, tile), :]
            downs.append([pltpu.make_async_copy(src, down_w.at[k], down_sems.at[k])])
    stream = downs + slab_chunks(here_ref, gate_hbm, up_hbm, gate_w, up_w, slab_sems, slabs)
    save = Saves(save_sems)

    start_all(first)
    start_all(stream[0])
    wait_all(first)
    start_all(scales[0])
    for copies in stream[1:ring]:
        start_all(copies)
    for copies in scales[1:]:
        start_all(copies)
    experts = local_count * exp_count
    used = 0
    for local in range(local_count):
        expert = here_ref[0] * local_count + local
        for pair in range(n // 2):
            hot = pair_one_hot(metas, expert, pair)
            weights = jnp.concatenate(pair_rows(metas, experts + expert, pair), axis=1)
            scale = jnp.sum(jnp.where(hot, weights, 0.0), axis=1, keepdims=True)

            def store(column, width, value):
                gp_ref[local, pl.ds(pair * 2 * CAP, 2 * CAP), pl.ds(column, width)] = value

            data.pack(here_ref, exp_count, slab, pair, hot.astype(BF16), scale, store)
        save(gp_ref.at[local], gp_hbm.at[local])
        wait_all(scales[local])
        for j in range(steps):
            wait_all(stream[used])
            units = pl.ds(j * tile, tile)
            hidden_grad = mm(gp_ref[local], down_w[used % ring], NT)
            ug_ref[local, :, units] = (hidden_grad * act_ref[local, :, units]).astype(BF16)
            gg_ref[local, :, units] = (hidden_grad * dact_ref[local, :, units]).astype(BF16)
            if used + ring < len(stream):
                start_all(stream[used + ring])
            used += 1
        save(gg_ref.at[local], gg_hbm.at[local])
        save(ug_ref.at[local], ug_hbm.at[local])
    slab_rows(n, here_ref, metas, gg_ref, ug_ref, gate_w, up_w, stream, used, out_ref,
              lambda src, s: save(src, outs[s]))
    wait_all(save.copies)


def hold_kernel(*refs):
    del refs


def hold(arrays, after):
    return pl.pallas_call(
        hold_kernel,
        out_shape=[jax.ShapeDtypeStruct(a.shape, a.dtype) for a in arrays],
        in_specs=anywhere(len(arrays) + len(after)),
        out_specs=anywhere(len(arrays)),
        input_output_aliases={k: k for k in range(len(arrays))},
        compiler_params=params(4),
        cost_estimate=cost(0, 0),
    )(*arrays, *after)


def weights_kernel(count, tile, *refs):
    lefts, refs = refs[:count], refs[count:]
    right, refs = refs[0], refs[1:]
    out_hbm, token_ref, left_ref, right_ref, out_ref, load_sems, save_sems = refs[-7:]
    token_ref[...] = jnp.zeros_like(token_ref)
    loads = [
        (pltpu.make_async_copy(lefts[e], left_ref.at[e], load_sems.at[0, e]),
         pltpu.make_async_copy(right.at[e], right_ref.at[e], load_sems.at[1, e]))
        for e in range(count)
    ]
    rows = left_ref.shape[2]
    cols = right_ref.shape[2]
    tiles = [(e, r, c) for e in range(count) for r in range(0, rows, tile) for c in range(0, cols, tile)]
    saves = []
    start_all(loads[0])
    for k, (e, r, c) in enumerate(tiles):
        if r == 0 and c == 0:
            wait_all(loads[e])
            if e + 1 < count:
                start_all(loads[e + 1])
        if k >= 2:
            saves[k - 2].wait()
        at = (pl.ds(r, min(tile, rows)), pl.ds(c, min(tile, cols)))
        out_ref[k % 2] = mm(left_ref[e, :, at[0]], right_ref[e, :, at[1]], TN).astype(BF16)
        saves.append(pltpu.make_async_copy(out_ref.at[k % 2], out_hbm.at[e, at[0], at[1]], save_sems.at[k % 2]))
        saves[k].start()
    wait_all(saves[-2:])


def weight_grad(lefts, right, after):
    count = len(lefts)
    slots, m = lefts[0].shape
    cols = right.shape[2]
    tile = 1024
    return pl.pallas_call(
        functools.partial(weights_kernel, count, tile),
        out_shape=[jax.ShapeDtypeStruct((count, m, cols), BF16), jax.ShapeDtypeStruct((8, 128), F32)],
        in_specs=hbm(count + 1) + anywhere(len(after)),
        out_specs=hbm(1) + vmem(1),
        scratch_shapes=[VM((count, slots, m), BF16), VM((count, slots, cols), BF16),
                        VM((2, min(tile, m), min(tile, cols)), BF16),
                        pltpu.SemaphoreType.DMA((2, count)), pltpu.SemaphoreType.DMA((2,))],
        compiler_params=params(28),
        cost_estimate=cost(2 * count * slots * m * cols, 2 * count * m * cols),
    )(*map(far, lefts), far(right), *after)


def gather_ctx(mine, n):
    return [lax.ppermute(mine, "ctx", shift(n, s)) for s in range(1, n)]


def exchange(received, exp_count):
    others = jnp.stack(received)
    return others, [lax.ppermute(others, "exp", shift(exp_count, dx)) for dx in range(1, exp_count)]


def siblings(parts, offset):
    pieces, arrays = [], []
    for dx, part in enumerate(parts):
        pieces += [(dx, 0, offset), (dx, 1, offset)]
        arrays += [part, lax.ppermute(part, "tp", shift(2, 1))]
    return pieces, arrays


def per_device(tokens, out_grad, expert_ids, gate_weights, gate_matrix, up_matrix, down_matrix):
    n = lax.axis_size("ctx")
    exp_count = lax.axis_size("exp")
    x = lax.axis_index("exp")
    c = lax.axis_index("tp")
    local_count, depth, hidden_units = gate_matrix.shape
    experts = local_count * exp_count
    block, _ = tokens.shape
    width = depth // (exp_count * 2)
    slots = n * CAP
    here = jnp.stack([x, c, (x * 2 + c) * width, 0]).astype(jnp.int32)

    names = jnp.arange(experts, dtype=jnp.int32)[:, None]
    chosen = [expert_ids[:, k][None, :] == names for k in range(expert_ids.shape[1])]
    member = functools.reduce(jnp.logical_or, chosen)
    before = jnp.arange(block)[:, None] <= jnp.arange(block)[None, :]
    order = jnp.dot(member.astype(BF16), before.astype(BF16), preferred_element_type=F32)
    slot = jnp.where(member, order - 1.0, -1.0)
    weight = sum(jnp.where(ch, gate_weights[:, k][None, :], 0.0) for k, ch in enumerate(chosen))
    meta = jnp.concatenate([slot, weight], axis=0)

    half = width // 256 * 128

    def mine(array, offset, size):
        return lax.dynamic_slice_in_dim(array, (x * 2 + c) * width + offset, size, axis=1)

    m = n - 1
    step = hold(gather_ctx(mine(tokens, 0, width), n) + gather_ctx(meta, n), [])
    t_ctx, metas = step[:m], [meta, *step[m:]]
    t_all, t_exp = exchange(t_ctx, exp_count)
    step = hold(gather_ctx(mine(out_grad, 0, half), n) + t_exp, [])
    g0, t_exp = step[:m], step[m:]
    t_pieces, t_arrays = siblings([t_all, *t_exp], 0)
    g0_all, g0_exp = exchange(g0, exp_count)
    g1 = gather_ctx(mine(out_grad, half, width - half), n)

    tile = min(512, hidden_units)
    fine = min(256, hidden_units)
    flops = 2 * local_count * slots * depth * hidden_units
    dma = pltpu.SemaphoreType.DMA
    stack = lambda cols, dtype: pltpu.HBM((slots, cols), dtype)
    near = lambda shape: pltpu.HBM(shape, BF16)

    def load_args(own, arrays):
        return [far(own), *arrays], [VM(a.shape, BF16) for a in [own, *arrays]]

    flat, staged = load_args(tokens, t_arrays)
    forward = []
    for local in range(local_count):
        forward.append(pl.pallas_call(
            functools.partial(forward_kernel, n, exp_count, t_pieces, width, fine, local),
            out_shape=(stack(depth, BF16), stack(hidden_units, BF16),
                       stack(hidden_units, F32), stack(hidden_units, F32),
                       jax.ShapeDtypeStruct((8, 128), F32)),
            in_specs=[SCALARS] + vmem(n) + anywhere(len(flat)) + hbm(2),
            out_specs=hbm(4) + vmem(1),
            scratch_shapes=staged + [VM((slots, depth), BF16), VM((slots, hidden_units), BF16)]
            + [VM((slots, hidden_units), F32)] * 2 + [VM((2, depth, fine), BF16)] * 2
            + [dma((len(flat),)), dma((2, 2)), dma((2 + 2 * (hidden_units // fine),))],
            compiler_params=params(34),
            cost_estimate=cost(2 * flops // local_count, 0),
        )(here, *metas, *flat, far(gate_matrix), far(up_matrix)))
        if local == 0:
            step = hold(g1 + g0_exp, forward[0][4:])
            g1, g0_exp = step[:m], step[m:]
            g1_all, g1_exp = exchange(g1, exp_count)
    xps, hiddens, acts, dacts, ends = zip(*forward)
    g1_exp = hold(g1_exp, ends[1:])
    g_pieces, g_arrays = siblings([g0_all, *g0_exp], 0)
    more_pieces, more_arrays = siblings([g1_all, *g1_exp], half)
    g_pieces += more_pieces
    g_arrays += more_arrays

    slabs = [(dx, dc) for dx in [*range(1, exp_count), 0] for dc in (1, 0)]
    at = [lax.rem(x + dx, exp_count) * 2 + lax.rem(c + dc, 2) for dx, dc in slabs]
    part = (n, block, width)
    units = (local_count, slots, hidden_units)
    ring = 3
    for k in range(0, len(g_arrays), 2 * exp_count):
        g_arrays[k:k + 2] = map(far, g_arrays[k:k + 2])
    flat, staged = load_args(out_grad, g_arrays)
    gp, gate_grad, up_grad, *outs = pl.pallas_call(
        functools.partial(
            backward_kernel, n, exp_count, g_pieces, width, tile, local_count, len(slabs)
        ),
        out_shape=[near((local_count, slots, depth)), near(units), near(units)]
        + [near(part)] * len(slabs),
        in_specs=[SCALARS] + vmem(n) + anywhere(len(flat)) + hbm(2 * local_count + 3),
        out_specs=hbm(3 + len(slabs)),
        scratch_shapes=staged
        + [VM(units, F32)] * 2 + [VM((local_count, slots, depth), BF16)] + [VM(units, BF16)] * 2
        + [VM((len(slabs), *part), BF16)] + [VM((ring, width, hidden_units), BF16)] * 2
        + [VM((ring, tile, depth), BF16), dma((len(flat),)), dma((2, local_count)),
           dma((2, ring)), dma((ring,)), dma((3 * local_count + len(slabs),))],
        compiler_params=params(54),
        cost_estimate=cost(3 * flops, 0),
    )(
        jnp.stack([x, c, *at]).astype(jnp.int32), *metas, *flat, *map(far, acts), *map(far, dacts),
        far(gate_matrix), far(up_matrix), far(down_matrix),
    )
    outs = dict(zip(slabs, outs))
    tp_sums = {dx: lax.ppermute(outs[dx, 1], "tp", shift(2, 1)) for dx in range(exp_count)}

    def chip_sum(dx, rows):
        return outs[dx, 0][rows].astype(F32) + tp_sums[dx][rows].astype(F32)

    parts = [slice(0, n // 2), slice(n // 2, n)]
    sent = [
        [chip_sum(dx, rows).astype(BF16) for dx in range(1, exp_count)] for rows in parts
    ]
    grad_gate, token = weight_grad(xps, gate_grad, sent[0])
    sent[1] = hold(sent[1], [token])
    arrived = [
        [lax.ppermute(a, "exp", shift(exp_count, dx + 1)) for dx, a in enumerate(group)]
        for group in sent
    ]
    final, rounded = None, []
    for k, rows in enumerate(parts):
        total = chip_sum(0, rows)
        for other in arrived[k]:
            total = total + other.astype(F32)
        rounded.append(total.astype(BF16))
        for j in range(total.shape[0]):
            s = rows.start + j + 1
            if s < n:
                term = lax.ppermute(rounded[k][j], "ctx", shift(n, -s)).astype(F32)
            else:
                term = total[j]
            final = term if final is None else final + term
        if k == 0:
            grad_up, token = weight_grad(xps, up_grad, [token, rounded[0]])
            arrived[1] = hold(arrived[1], [token])
    grad_tokens = final.astype(BF16)

    grad_down, _ = weight_grad(hiddens, gp, [token, rounded[1]])
    return (grad_gate, grad_up, grad_down, grad_tokens)


def solution(mesh):
    in_specs = (
        P(("groups", "ctx"), None),
        P(("groups", "ctx"), None),
        P(("groups", "ctx"), None),
        P(("groups", "ctx"), None),
        P("exp", None, ("ctx", "tp")),
        P("exp", None, ("ctx", "tp")),
        P("exp", ("ctx", "tp"), None),
    )
    out_specs = (
        P(("groups", "exp"), None, ("ctx", "tp")),
        P(("groups", "exp"), None, ("ctx", "tp")),
        P(("groups", "exp"), ("ctx", "tp"), None),
        P(("groups", "ctx"), ("exp", "tp")),
    )
    return jax.shard_map(
        per_device, mesh=mesh, in_specs=in_specs, out_specs=out_specs, check_vma=False
    )
```

```python
import functools

import jax
import jax.numpy as jnp
from jax import lax
from jax.experimental import pallas as pl
from jax.experimental.pallas import tpu as pltpu
from jax.sharding import PartitionSpec as P

CAP = 72
VM = pltpu.VMEM
F32 = jnp.float32
BF16 = jnp.bfloat16
NN = (((1,), (0,)), ((), ()))
NT = (((1,), (1,)), ((), ()))
TN = (((0,), (0,)), ((), ()))


def mm(a, b, dims):
    return lax.dot_general(a, b, dims, preferred_element_type=F32)


def params(mib):
    return pltpu.CompilerParams(vmem_limit_bytes=mib * 1024 * 1024)


def cost(flops, nbytes):
    return pl.CostEstimate(flops=int(flops), bytes_accessed=int(nbytes), transcendentals=0)


def vmem(count):
    return [pl.BlockSpec(memory_space=VM)] * count


def far(array):
    return pltpu.with_memory_space_constraint(array, pltpu.HBM)


def anywhere(count):
    return [pl.BlockSpec(memory_space=pl.ANY)] * count


def hbm(count):
    return [pl.BlockSpec(memory_space=pltpu.HBM)] * count


SCALARS = pl.BlockSpec(memory_space=pltpu.SMEM)


def shift(count, by):
    return [(i, (i + by) % count) for i in range(count)]


def pair_rows(metas, row, pair):
    first = metas[2 * pair][pl.ds(row, 1), :]
    second = metas[2 * pair + 1][pl.ds(row, 1), :]
    return first, second


def pair_one_hot(metas, expert, pair):
    first, second = pair_rows(metas, expert, pair)
    second = jnp.where(second >= 0, second + CAP, second)
    slot = jnp.concatenate([first, second], axis=1)
    rows = lax.broadcasted_iota(jnp.int32, (2 * CAP, slot.shape[1]), 0).astype(F32)
    return rows == slot


class Gathered:
    def __init__(self, refs, pieces):
        self.own = refs[0]
        self.pieces = list(zip(pieces, refs[1:]))

    def pack(self, here, exp_count, slab, pair, hot, scale, store):
        for (dx, dc, offset), ref in self.pieces:
            x = lax.rem(here[0] + exp_count - dx, exp_count)
            c = lax.rem(here[1] + dc, 2)
            width = ref.shape[2]
            column = pl.multiple_of((x * 2 + c) * slab + offset, 128)
            if pair == 0:
                rows = jnp.concatenate([self.own[:, pl.ds(column, width)], ref[0]], axis=0)
            else:
                rows = jnp.concatenate([ref[2 * pair - 1], ref[2 * pair]], axis=0)
            packed = mm(hot, rows, NN)
            if scale is not None:
                packed = packed * scale
            store(column, width, packed.astype(BF16))


def start_all(copies):
    for copy in copies:
        copy.start()


def wait_all(copies):
    for copy in copies:
        copy.wait()


def fetch_kernel(parts, *refs):
    srcs, dsts, token_ref, sems = refs[:2], refs[-4:-2], refs[-2], refs[-1]
    token_ref[...] = jnp.zeros_like(token_ref)
    copies = []
    for k, (src, dst) in enumerate(zip(srcs, dsts)):
        rows = src.shape[1] // parts
        for e in range(src.shape[0]):
            for p in range(parts):
                at = (e, pl.ds(p * rows, rows))
                copies.append(pltpu.make_async_copy(src.at[at], dst.at[at], sems.at[k, e, p]))
    start_all(copies)
    wait_all(copies)


def fetch(gate, up, after):
    parts = 2
    return pl.pallas_call(
        functools.partial(fetch_kernel, parts),
        out_shape=[VM(gate.shape, BF16), VM(up.shape, BF16), jax.ShapeDtypeStruct((8, 128), F32)],
        in_specs=hbm(2) + anywhere(len(after)),
        out_specs=vmem(3),
        scratch_shapes=[pltpu.SemaphoreType.DMA((2, gate.shape[0], parts))],
        compiler_params=params(4),
        cost_estimate=cost(0, 8 * gate.size),
    )(far(gate), far(up), *after)


class Saves:
    def __init__(self, sems):
        self.sems, self.copies = sems, []

    def __call__(self, src, dst):
        copy = pltpu.make_async_copy(src, dst, self.sems.at[len(self.copies)])
        copy.start()
        self.copies.append(copy)
        return copy


def load_all(srcs, dsts, sems):
    return [pltpu.make_async_copy(src, dst, sems.at[k]) for k, (src, dst) in enumerate(zip(srcs, dsts))]


def forward_kernel(n, exp_count, pieces, slab, tile, local, here_ref, *refs):
    metas, refs = refs[:n], refs[n:]
    loads, refs = refs[:1 + len(pieces)], refs[1 + len(pieces):]
    gate_w, up_w, xp_out, hid_out, act_out, dact_out, token_ref = refs[:7]
    staged, refs = refs[7:7 + len(loads)], refs[7 + len(loads):]
    token_ref[...] = jnp.zeros_like(token_ref)
    xp_ref, hid_ref, act_ref, dact_ref, load_sems, save_sems = refs
    data = Gathered(staged, pieces)
    steps = gate_w.shape[2] // tile
    expert = here_ref[0] * gate_w.shape[0] + local

    first = load_all(loads, staged, load_sems)
    save = Saves(save_sems)
    start_all(first)
    wait_all(first)
    for pair in range(n // 2):
        hot = pair_one_hot(metas, expert, pair).astype(BF16)

        def store(column, width, value):
            xp_ref[pl.ds(pair * 2 * CAP, 2 * CAP), pl.ds(column, width)] = value

        data.pack(here_ref, exp_count, slab, pair, hot, None, store)
    save(xp_ref, xp_out)
    for j in range(steps):
        units = pl.ds(j * tile, tile)
        rows = xp_ref[...]
        gate = mm(rows, gate_w[local, :, units], NN)
        up = mm(rows, up_w[local, :, units], NN)
        sig = jax.nn.sigmoid(gate)
        act = gate * sig
        hid_ref[:, units] = (act * up).astype(BF16)
        act_ref[:, units] = act.astype(BF16)
        dact_ref[:, units] = (up * sig * (1.0 + gate * (1.0 - sig))).astype(BF16)
        save(act_ref.at[:, units], act_out.at[:, units])
        save(dact_ref.at[:, units], dact_out.at[:, units])
    save(hid_ref, hid_out)
    wait_all(save.copies)


def slab_chunks(here_ref, gate_hbm, up_hbm, gate_w, up_w, sems, slabs):
    ring, width, _ = gate_w.shape
    chunks = []
    for s in range(slabs):
        rows = pl.ds(pl.multiple_of(here_ref[2 + s] * width, 128), width)
        for e in range(gate_hbm.shape[0]):
            k = len(chunks) % ring
            chunks.append([
                pltpu.make_async_copy(src.at[e, rows, :], dst.at[k], sems.at[m, k])
                for m, (src, dst) in enumerate(((gate_hbm, gate_w), (up_hbm, up_w)))
            ])
    return chunks


def slab_rows(n, slabs, here_ref, metas, gg_ref, ug_ref, gate_w, up_w, stream, used, out_ref, save):
    local_count = gg_ref.shape[0]
    ring = gate_w.shape[0]
    begun = used
    saves = []
    for s in range(slabs):
        if s >= 2:
            saves[s - 2].wait()
        terms = []
        for local in range(local_count):
            wait_all(stream[used])
            k = (used - begun) % ring
            term = mm(gg_ref[local], gate_w[k], NT) + mm(ug_ref[local], up_w[k], NT)
            terms.append(term.astype(BF16))
            if used + ring < len(stream):
                start_all(stream[used + ring])
            used += 1
        for pair in range(n // 2):
            total = None
            for local, term in enumerate(terms):
                expert = here_ref[0] * local_count + local
                hot = pair_one_hot(metas, expert, pair).astype(BF16)
                part = mm(hot, term[pair * 2 * CAP:(pair + 1) * 2 * CAP], TN)
                total = part if total is None else total + part
            half = total.shape[0] // 2
            for j in range(2):
                out_ref[s % 2, (2 * pair + j - 1) % n] = total[j * half:(j + 1) * half].astype(BF16)
        saves.append(save(out_ref.at[s % 2], s))


def backward_kernel(n, exp_count, pieces, slab, tile, local_count, slabs, here_ref, *refs):
    metas, refs = refs[:n], refs[n:]
    loads, refs = refs[:1 + len(pieces)], refs[1 + len(pieces):]
    act_hbm, refs = refs[:2 * local_count], refs[2 * local_count:]
    kept, refs = refs[:2 * local_count], refs[2 * local_count:]
    gate_hbm, up_hbm, down_hbm, gp_ref, gg_ref, ug_ref, xp_ref, hid_ref = refs[:8]
    outs, refs = refs[8:8 + slabs], refs[8 + slabs:]
    staged, refs = refs[:len(loads)], refs[len(loads):]
    (act_ref, dact_ref, out_ref, gate_w, up_w, down_w,
     load_sems, act_sems, slab_sems, down_sems, save_sems, keep_sems) = refs
    data = Gathered(staged, pieces)
    steps = gg_ref.shape[2] // tile
    ring = down_w.shape[0]

    first = load_all(loads, staged, load_sems)
    scales = []
    for e in range(local_count):
        scales.append([
            pltpu.make_async_copy(act_hbm[e], act_ref.at[e], act_sems.at[0, e]),
            pltpu.make_async_copy(act_hbm[local_count + e], dact_ref.at[e], act_sems.at[1, e]),
        ])
    downs = []
    for e in range(local_count):
        for j in range(steps):
            k = len(downs) % ring
            src = down_hbm.at[e, pl.ds(j * tile, tile), :]
            downs.append([pltpu.make_async_copy(src, down_w.at[k], down_sems.at[k])])
    stream = downs + slab_chunks(here_ref, gate_hbm, up_hbm, gate_w, up_w, slab_sems, slabs)
    save = Saves(save_sems)

    start_all(first)
    start_all(stream[0])
    wait_all(first)
    start_all(scales[0])
    for copies in stream[1:ring]:
        start_all(copies)
    for copies in scales[1:]:
        start_all(copies)
    experts = local_count * exp_count
    used = 0
    for local in range(local_count):
        expert = here_ref[0] * local_count + local
        for pair in range(n // 2):
            hot = pair_one_hot(metas, expert, pair)
            weights = jnp.concatenate(pair_rows(metas, experts + expert, pair), axis=1)
            scale = jnp.sum(jnp.where(hot, weights, 0.0), axis=1, keepdims=True)

            def store(column, width, value):
                gp_ref[local, pl.ds(pair * 2 * CAP, 2 * CAP), pl.ds(column, width)] = value

            data.pack(here_ref, exp_count, slab, pair, hot.astype(BF16), scale, store)
        wait_all(scales[local])
        for j in range(steps):
            wait_all(stream[used])
            units = pl.ds(j * tile, tile)
            hidden_grad = mm(gp_ref[local], down_w[used % ring], NT)
            ug_ref[local, :, units] = (hidden_grad * act_ref[local, :, units].astype(F32)).astype(BF16)
            gg_ref[local, :, units] = (hidden_grad * dact_ref[local, :, units].astype(F32)).astype(BF16)
            if used + ring < len(stream):
                start_all(stream[used + ring])
            used += 1
    keeps = []
    for k, (refs, dst) in enumerate(((kept[:local_count], xp_ref), (kept[local_count:], hid_ref))):
        for e, src in enumerate(refs):
            keeps.append(pltpu.make_async_copy(src, dst.at[e], keep_sems.at[k, e]))
    start_all(keeps)
    slab_rows(n, slabs, here_ref, metas, gg_ref, ug_ref, gate_w, up_w, stream, used, out_ref,
              lambda src, s: save(src, outs[s]))
    wait_all(save.copies[-2:] + keeps)


def hold_kernel(*refs):
    del refs


def hold(arrays, after):
    return pl.pallas_call(
        hold_kernel,
        out_shape=[jax.ShapeDtypeStruct(a.shape, a.dtype) for a in arrays],
        in_specs=anywhere(len(arrays) + len(after)),
        out_specs=anywhere(len(arrays)),
        input_output_aliases={k: k for k in range(len(arrays))},
        compiler_params=params(4),
        cost_estimate=cost(0, 0),
    )(*arrays, *after)


def weights_kernel(tile, left_ref, right_ref, *refs):
    out_hbm, token_ref, out_ref, save_sems = refs[-4:]
    token_ref[...] = jnp.zeros_like(token_ref)
    count, _, rows = left_ref.shape
    cols = right_ref.shape[2]
    saves = []
    for e in range(count):
        for r in range(0, rows, tile):
            for c in range(0, cols, tile):
                k = len(saves)
                if k >= 2:
                    saves[k - 2].wait()
                at = (pl.ds(r, min(tile, rows)), pl.ds(c, min(tile, cols)))
                out_ref[k % 2] = mm(left_ref[e, :, at[0]], right_ref[e, :, at[1]], TN).astype(BF16)
                dst = out_hbm.at[e, at[0], at[1]]
                saves.append(pltpu.make_async_copy(out_ref.at[k % 2], dst, save_sems.at[k % 2]))
                saves[k].start()
    wait_all(saves[-2:])


def weight_grad(left, right, after):
    count, slots, m = left.shape
    cols = right.shape[2]
    tile = 1024
    return pl.pallas_call(
        functools.partial(weights_kernel, tile),
        out_shape=[jax.ShapeDtypeStruct((count, m, cols), BF16), jax.ShapeDtypeStruct((8, 128), F32)],
        in_specs=vmem(2) + anywhere(len(after)),
        out_specs=hbm(1) + vmem(1),
        scratch_shapes=[VM((2, min(tile, m), min(tile, cols)), BF16), pltpu.SemaphoreType.DMA((2,))],
        compiler_params=params(16),
        cost_estimate=cost(2 * count * slots * m * cols, 2 * count * m * cols),
    )(left, right, *after)


def gather_ctx(mine, n):
    return [lax.ppermute(mine, "ctx", shift(n, s)) for s in range(1, n)]


def exchange(received, exp_count):
    others = jnp.stack(received)
    return others, [lax.ppermute(others, "exp", shift(exp_count, dx)) for dx in range(1, exp_count)]


def siblings(parts, offset):
    pieces, arrays = [], []
    for dx, part in enumerate(parts):
        pieces += [(dx, 0, offset), (dx, 1, offset)]
        arrays += [part, lax.ppermute(part, "tp", shift(2, 1))]
    return pieces, arrays


def per_device(tokens, out_grad, expert_ids, gate_weights, gate_matrix, up_matrix, down_matrix):
    n = lax.axis_size("ctx")
    exp_count = lax.axis_size("exp")
    x = lax.axis_index("exp")
    c = lax.axis_index("tp")
    local_count, depth, hidden_units = gate_matrix.shape
    experts = local_count * exp_count
    block, _ = tokens.shape
    width = depth // (exp_count * 2)
    slots = n * CAP
    here = jnp.stack([x, c, (x * 2 + c) * width, 0]).astype(jnp.int32)

    names = jnp.arange(experts, dtype=jnp.int32)[:, None]
    chosen = [expert_ids[:, k][None, :] == names for k in range(expert_ids.shape[1])]
    member = functools.reduce(jnp.logical_or, chosen)
    before = jnp.arange(block)[:, None] <= jnp.arange(block)[None, :]
    order = jnp.dot(member.astype(BF16), before.astype(BF16), preferred_element_type=F32)
    slot = jnp.where(member, order - 1.0, -1.0)
    weight = sum(jnp.where(ch, gate_weights[:, k][None, :], 0.0) for k, ch in enumerate(chosen))
    meta = jnp.concatenate([slot, weight], axis=0)

    half = width // 256 * 128

    def mine(array, offset, size):
        return lax.dynamic_slice_in_dim(array, (x * 2 + c) * width + offset, size, axis=1)

    m = n - 1
    step = hold(gather_ctx(mine(tokens, 0, width), n) + gather_ctx(meta, n), [])
    t_ctx, metas = step[:m], [meta, *step[m:]]
    t_all, t_exp = exchange(t_ctx, exp_count)
    gate_v, up_v, token = fetch(gate_matrix, up_matrix, t_ctx)
    step = hold(gather_ctx(mine(out_grad, 0, half), n) + t_exp, [token])
    g0, t_exp = step[:m], step[m:]
    t_pieces, t_arrays = siblings([t_all, *t_exp], 0)
    g0_all, g0_exp = exchange(g0, exp_count)
    g1 = gather_ctx(mine(out_grad, half, width - half), n)

    tile = min(512, hidden_units)
    flops = 2 * local_count * slots * depth * hidden_units
    dma = pltpu.SemaphoreType.DMA
    stack = lambda cols, dtype: pltpu.HBM((slots, cols), dtype)
    near = lambda shape: pltpu.HBM(shape, BF16)

    def load_args(own, arrays):
        return [far(own), *arrays], [VM(a.shape, BF16) for a in [own, *arrays]]

    flat, staged = load_args(tokens, t_arrays)
    forward = []
    for local in range(local_count):
        forward.append(pl.pallas_call(
            functools.partial(forward_kernel, n, exp_count, t_pieces, width, tile, local),
            out_shape=(stack(depth, BF16), stack(hidden_units, BF16),
                       stack(hidden_units, BF16), stack(hidden_units, BF16),
                       jax.ShapeDtypeStruct((8, 128), F32)),
            in_specs=[SCALARS] + vmem(n) + anywhere(len(flat)) + vmem(2),
            out_specs=hbm(4) + vmem(1),
            scratch_shapes=staged + [VM((slots, depth), BF16), VM((slots, hidden_units), BF16)]
            + [VM((slots, hidden_units), BF16)] * 2
            + [dma((len(flat),)), dma((2 + 2 * (hidden_units // tile),))],
            compiler_params=params(16 if n <= 8 else 28),
            cost_estimate=cost(2 * flops // local_count, 0),
        )(here, *metas, *flat, gate_v, up_v))
        if local == 0:
            step = hold(g1 + g0_exp, forward[0][4:])
            g1, g0_exp = step[:m], step[m:]
            g1_all, g1_exp = exchange(g1, exp_count)
    xps, hiddens, acts, dacts, ends = zip(*forward)
    g1_exp = hold(g1_exp, ends[1:])
    g_pieces, g_arrays = siblings([g0_all, *g0_exp], 0)
    more_pieces, more_arrays = siblings([g1_all, *g1_exp], half)
    g_pieces += more_pieces
    g_arrays += more_arrays

    slabs = [(dx, dc) for dx in [*range(1, exp_count), 0] for dc in (1, 0)]
    at = [lax.rem(x + dx, exp_count) * 2 + lax.rem(c + dc, 2) for dx, dc in slabs]
    part = (n, block, width)
    units = (local_count, slots, hidden_units)
    ring = 3
    for k in range(0, len(g_arrays), 2 * exp_count):
        g_arrays[k:k + 2] = map(far, g_arrays[k:k + 2])
    flat, staged = load_args(out_grad, g_arrays)
    gp, gate_grad, up_grad, xp, hidden, *outs = pl.pallas_call(
        functools.partial(
            backward_kernel, n, exp_count, g_pieces, width, tile, local_count, len(slabs)
        ),
        out_shape=[VM((local_count, slots, depth), BF16), VM(units, BF16), VM(units, BF16)]
        + [VM((local_count, slots, depth), BF16), VM(units, BF16)] + [near(part)] * len(slabs),
        in_specs=[SCALARS] + vmem(n) + anywhere(len(flat)) + hbm(4 * local_count + 3),
        out_specs=vmem(5) + hbm(len(slabs)),
        scratch_shapes=staged
        + [VM(units, BF16)] * 2
        + [VM((2, *part), BF16)] + [VM((ring, width, hidden_units), BF16)] * 2
        + [VM((ring, tile, depth), BF16), dma((len(flat),)), dma((2, local_count)),
           dma((2, ring)), dma((ring,)), dma((len(slabs),)), dma((2, local_count))],
        compiler_params=params(40 if n <= 8 else 48),
        cost_estimate=cost(3 * flops, 0),
    )(
        jnp.stack([x, c, *at]).astype(jnp.int32), *metas, *flat, *map(far, acts), *map(far, dacts),
        *map(far, xps), *map(far, hiddens),
        far(gate_matrix), far(up_matrix), far(down_matrix),
    )
    outs = dict(zip(slabs, outs))
    tp_sums = {dx: lax.ppermute(outs[dx, 1], "tp", shift(2, 1)) for dx in range(exp_count)}

    def chip_sum(dx, rows):
        return outs[dx, 0][rows].astype(F32) + tp_sums[dx][rows].astype(F32)

    parts = [slice(0, n // 2), slice(n // 2, n)]
    sent = [
        [chip_sum(dx, rows).astype(BF16) for dx in range(1, exp_count)] for rows in parts
    ]
    grad_gate, token = weight_grad(xp, gate_grad, sent[0])
    sent[1] = hold(sent[1], [token])
    arrived = [
        [lax.ppermute(a, "exp", shift(exp_count, dx + 1)) for dx, a in enumerate(group)]
        for group in sent
    ]
    final, rounded = None, []
    for k, rows in enumerate(parts):
        total = chip_sum(0, rows)
        for other in arrived[k]:
            total = total + other.astype(F32)
        rounded.append(total.astype(BF16))
        for j in range(total.shape[0]):
            s = rows.start + j + 1
            if s < n:
                term = lax.ppermute(rounded[k][j], "ctx", shift(n, -s)).astype(F32)
            else:
                term = total[j]
            final = term if final is None else final + term
        if k == 0:
            grad_up, token = weight_grad(xp, up_grad, [token, rounded[0]])
            arrived[1] = hold(arrived[1], [token])
    grad_tokens = final.astype(BF16)

    grad_down, _ = weight_grad(hidden, gp, [token, rounded[1]])
    return (grad_gate, grad_up, grad_down, grad_tokens)


def solution(mesh):
    in_specs = (
        P(("groups", "ctx"), None),
        P(("groups", "ctx"), None),
        P(("groups", "ctx"), None),
        P(("groups", "ctx"), None),
        P("exp", None, ("ctx", "tp")),
        P("exp", None, ("ctx", "tp")),
        P("exp", ("ctx", "tp"), None),
    )
    out_specs = (
        P(("groups", "exp"), None, ("ctx", "tp")),
        P(("groups", "exp"), None, ("ctx", "tp")),
        P(("groups", "exp"), ("ctx", "tp"), None),
        P(("groups", "ctx"), ("exp", "tp")),
    )
    return jax.shard_map(
        per_device, mesh=mesh, in_specs=in_specs, out_specs=out_specs, check_vma=False
    )
```

```python
import functools

import jax
import jax.numpy as jnp
from jax import lax
from jax.experimental import pallas as pl
from jax.experimental.pallas import tpu as pltpu
from jax.sharding import PartitionSpec as P

CAP = 72
VM = pltpu.VMEM
F32 = jnp.float32
BF16 = jnp.bfloat16
NN = (((1,), (0,)), ((), ()))
NT = (((1,), (1,)), ((), ()))
TN = (((0,), (0,)), ((), ()))


def mm(a, b, dims):
    return lax.dot_general(a, b, dims, preferred_element_type=F32)


def params(mib):
    return pltpu.CompilerParams(vmem_limit_bytes=mib * 1024 * 1024)


def cost(flops, nbytes):
    return pl.CostEstimate(flops=int(flops), bytes_accessed=int(nbytes), transcendentals=0)


def vmem(count):
    return [pl.BlockSpec(memory_space=VM)] * count


def far(array):
    return pltpu.with_memory_space_constraint(array, pltpu.HBM)


def anywhere(count):
    return [pl.BlockSpec(memory_space=pl.ANY)] * count


def hbm(count):
    return [pl.BlockSpec(memory_space=pltpu.HBM)] * count


SCALARS = pl.BlockSpec(memory_space=pltpu.SMEM)


def shift(count, by):
    return [(i, (i + by) % count) for i in range(count)]


def pair_rows(metas, row, pair):
    first = metas[2 * pair][pl.ds(row, 1), :]
    second = metas[2 * pair + 1][pl.ds(row, 1), :]
    return first, second


def pair_one_hot(metas, expert, pair):
    first, second = pair_rows(metas, expert, pair)
    second = jnp.where(second >= 0, second + CAP, second)
    slot = jnp.concatenate([first, second], axis=1)
    rows = lax.broadcasted_iota(jnp.int32, (2 * CAP, slot.shape[1]), 0).astype(F32)
    return rows == slot


class Gathered:
    def __init__(self, refs, pieces):
        self.own = refs[0]
        self.pieces = list(zip(pieces, refs[1:]))

    def pack(self, here, exp_count, slab, pair, hot, scale, store):
        for (dx, dc, offset), ref in self.pieces:
            x = lax.rem(here[0] + exp_count - dx, exp_count)
            c = lax.rem(here[1] + dc, 2)
            width = ref.shape[2]
            column = pl.multiple_of((x * 2 + c) * slab + offset, 128)
            if pair == 0:
                rows = jnp.concatenate([self.own[:, pl.ds(column, width)], ref[0]], axis=0)
            else:
                rows = jnp.concatenate([ref[2 * pair - 1], ref[2 * pair]], axis=0)
            packed = mm(hot, rows, NN)
            if scale is not None:
                packed = packed * scale
            store(column, width, packed.astype(BF16))


def start_all(copies):
    for copy in copies:
        copy.start()


def wait_all(copies):
    for copy in copies:
        copy.wait()


def fetch_kernel(parts, *refs):
    srcs, dsts, token_ref, sems = refs[:2], refs[-4:-2], refs[-2], refs[-1]
    token_ref[...] = jnp.zeros_like(token_ref)
    copies = []
    for k, (src, dst) in enumerate(zip(srcs, dsts)):
        rows = src.shape[1] // parts
        for e in range(src.shape[0]):
            for p in range(parts):
                at = (e, pl.ds(p * rows, rows))
                copies.append(pltpu.make_async_copy(src.at[at], dst.at[at], sems.at[k, e, p]))
    start_all(copies)
    wait_all(copies)


def fetch(gate, up, after):
    parts = 2
    return pl.pallas_call(
        functools.partial(fetch_kernel, parts),
        out_shape=[VM(gate.shape, BF16), VM(up.shape, BF16), jax.ShapeDtypeStruct((8, 128), F32)],
        in_specs=hbm(2) + anywhere(len(after)),
        out_specs=vmem(3),
        scratch_shapes=[pltpu.SemaphoreType.DMA((2, gate.shape[0], parts))],
        compiler_params=params(4),
        cost_estimate=cost(0, 8 * gate.size),
    )(far(gate), far(up), *after)


class Saves:
    def __init__(self, sems):
        self.sems, self.copies = sems, []

    def __call__(self, src, dst):
        copy = pltpu.make_async_copy(src, dst, self.sems.at[len(self.copies)])
        copy.start()
        self.copies.append(copy)
        return copy


def forward_kernel(n, exp_count, pieces, slab, tile, local, here_ref, *refs):
    metas, refs = refs[:n], refs[n:]
    loads, refs = refs[:1 + len(pieces)], refs[1 + len(pieces):]
    gate_w, up_w, xp_out, hid_out, act_out, dact_out, token_ref = refs[:7]
    refs = refs[7:]
    token_ref[...] = jnp.zeros_like(token_ref)
    xp_ref, hid_ref, act_ref, dact_ref, save_sems = refs
    data = Gathered(loads, pieces)
    steps = gate_w.shape[2] // tile
    expert = here_ref[0] * gate_w.shape[0] + local

    save = Saves(save_sems)
    for pair in range(n // 2):
        hot = pair_one_hot(metas, expert, pair).astype(BF16)

        def store(column, width, value):
            xp_ref[pl.ds(pair * 2 * CAP, 2 * CAP), pl.ds(column, width)] = value

        data.pack(here_ref, exp_count, slab, pair, hot, None, store)
    save(xp_ref, xp_out)
    for j in range(steps):
        units = pl.ds(j * tile, tile)
        rows = xp_ref[...]
        gate = mm(rows, gate_w[local, :, units], NN)
        up = mm(rows, up_w[local, :, units], NN)
        sig = jax.nn.sigmoid(gate)
        act = gate * sig
        hid_ref[:, units] = (act * up).astype(BF16)
        act_ref[:, units] = act.astype(BF16)
        dact_ref[:, units] = (up * sig * (1.0 + gate * (1.0 - sig))).astype(BF16)
        save(act_ref.at[:, units], act_out.at[:, units])
        save(dact_ref.at[:, units], dact_out.at[:, units])
    save(hid_ref, hid_out)
    wait_all(save.copies)


def slab_chunks(here_ref, gate_hbm, up_hbm, both_w, sems, slabs):
    ring, width, _ = both_w.shape
    units = gate_hbm.shape[2]
    chunks = []
    for s in range(slabs):
        rows = pl.ds(pl.multiple_of(here_ref[2 + s] * width, 128), width)
        for e in range(gate_hbm.shape[0]):
            k = len(chunks) % ring
            chunks.append([
                pltpu.make_async_copy(
                    src.at[e, rows, :], both_w.at[k, :, pl.ds(m * units, units)], sems.at[m, k]
                )
                for m, src in enumerate((gate_hbm, up_hbm))
            ])
    return chunks


def slab_rows(n, slabs, here_ref, metas, gu_ref, both_w, stream, used, out_ref, save):
    local_count = gu_ref.shape[0]
    ring = both_w.shape[0]
    begun = used
    saves = []
    for s in range(slabs):
        if s >= 2:
            saves[s - 2].wait()
        terms = []
        for local in range(local_count):
            wait_all(stream[used])
            k = (used - begun) % ring
            terms.append(mm(gu_ref[local], both_w[k], NT).astype(BF16))
            if used + ring < len(stream):
                start_all(stream[used + ring])
            used += 1
        for pair in range(n // 2):
            total = None
            for local, term in enumerate(terms):
                expert = here_ref[0] * local_count + local
                hot = pair_one_hot(metas, expert, pair).astype(BF16)
                part = mm(hot, term[pair * 2 * CAP:(pair + 1) * 2 * CAP], TN)
                total = part if total is None else total + part
            half = total.shape[0] // 2
            for j in range(2):
                out_ref[s % 2, (2 * pair + j - 1) % n] = total[j * half:(j + 1) * half].astype(BF16)
        saves.append(save(out_ref.at[s % 2], s))


def backward_kernel(n, exp_count, pieces, slab, tile, local_count, slabs, here_ref, *refs):
    metas, refs = refs[:n], refs[n:]
    loads, refs = refs[:1 + len(pieces)], refs[1 + len(pieces):]
    act_hbm, refs = refs[:2 * local_count], refs[2 * local_count:]
    kept, refs = refs[:2 * local_count], refs[2 * local_count:]
    gate_hbm, up_hbm, down_hbm, gp_ref, gu_ref, xp_ref, hid_ref = refs[:7]
    outs, refs = refs[7:7 + slabs], refs[7 + slabs:]
    (act_ref, dact_ref, out_ref, both_w, down_w,
     act_sems, slab_sems, down_sems, save_sems, keep_sems) = refs
    data = Gathered(loads, pieces)
    hidden_units = gu_ref.shape[2] // 2
    steps = hidden_units // tile
    ring = down_w.shape[0]

    scales = []
    for e in range(local_count):
        scales.append([
            pltpu.make_async_copy(act_hbm[e], act_ref.at[e], act_sems.at[0, e]),
            pltpu.make_async_copy(act_hbm[local_count + e], dact_ref.at[e], act_sems.at[1, e]),
        ])
    downs = []
    for e in range(local_count):
        for j in range(steps):
            k = len(downs) % ring
            src = down_hbm.at[e, pl.ds(j * tile, tile), :]
            downs.append([pltpu.make_async_copy(src, down_w.at[k], down_sems.at[k])])
    stream = downs + slab_chunks(here_ref, gate_hbm, up_hbm, both_w, slab_sems, slabs)
    save = Saves(save_sems)

    start_all(stream[0])
    start_all(scales[0])
    for copies in stream[1:ring]:
        start_all(copies)
    for copies in scales[1:]:
        start_all(copies)
    experts = local_count * exp_count
    used = 0
    for local in range(local_count):
        expert = here_ref[0] * local_count + local
        for pair in range(n // 2):
            hot = pair_one_hot(metas, expert, pair)
            weights = jnp.concatenate(pair_rows(metas, experts + expert, pair), axis=1)
            scale = jnp.sum(jnp.where(hot, weights, 0.0), axis=1, keepdims=True)

            def store(column, width, value):
                gp_ref[local, pl.ds(pair * 2 * CAP, 2 * CAP), pl.ds(column, width)] = value

            data.pack(here_ref, exp_count, slab, pair, hot.astype(BF16), scale, store)
        wait_all(scales[local])
        for j in range(steps):
            wait_all(stream[used])
            units = pl.ds(j * tile, tile)
            hidden_grad = mm(gp_ref[local], down_w[used % ring], NT)
            later = pl.ds(hidden_units + j * tile, tile)
            gu_ref[local, :, later] = (hidden_grad * act_ref[local, :, units].astype(F32)).astype(BF16)
            gu_ref[local, :, units] = (hidden_grad * dact_ref[local, :, units].astype(F32)).astype(BF16)
            if used + ring < len(stream):
                start_all(stream[used + ring])
            used += 1
    keeps = []
    for k, (refs, dst) in enumerate(((kept[:local_count], xp_ref), (kept[local_count:], hid_ref))):
        for e, src in enumerate(refs):
            keeps.append(pltpu.make_async_copy(src, dst.at[e], keep_sems.at[k, e]))
    start_all(keeps)
    slab_rows(n, slabs, here_ref, metas, gu_ref, both_w, stream, used, out_ref,
              lambda src, s: save(src, outs[s]))
    wait_all(save.copies[-2:] + keeps)


def hold_kernel(*refs):
    del refs


def hold(arrays, after):
    return pl.pallas_call(
        hold_kernel,
        out_shape=[jax.ShapeDtypeStruct(a.shape, a.dtype) for a in arrays],
        in_specs=anywhere(len(arrays) + len(after)),
        out_specs=anywhere(len(arrays)),
        input_output_aliases={k: k for k in range(len(arrays))},
        compiler_params=params(4),
        cost_estimate=cost(0, 0),
    )(*arrays, *after)


def weights_kernel(tile, begin, cols, left_ref, right_ref, *refs):
    out_hbm, token_ref, out_ref, save_sems = refs[-4:]
    token_ref[...] = jnp.zeros_like(token_ref)
    count, _, rows = left_ref.shape
    saves = []
    for e in range(count):
        for r in range(0, rows, tile):
            for c in range(0, cols, tile):
                k = len(saves)
                if k >= 2:
                    saves[k - 2].wait()
                at = (pl.ds(r, min(tile, rows)), pl.ds(c, min(tile, cols)))
                right = right_ref[e, :, pl.ds(begin + c, min(tile, cols))]
                out_ref[k % 2] = mm(left_ref[e, :, at[0]], right, TN).astype(BF16)
                dst = out_hbm.at[e, at[0], at[1]]
                saves.append(pltpu.make_async_copy(out_ref.at[k % 2], dst, save_sems.at[k % 2]))
                saves[k].start()
    wait_all(saves[-2:])


def weight_grad(left, right, begin, cols, after):
    count, slots, m = left.shape
    tile = 1024
    return pl.pallas_call(
        functools.partial(weights_kernel, tile, begin, cols),
        out_shape=[jax.ShapeDtypeStruct((count, m, cols), BF16), jax.ShapeDtypeStruct((8, 128), F32)],
        in_specs=vmem(2) + anywhere(len(after)),
        out_specs=hbm(1) + vmem(1),
        scratch_shapes=[VM((2, min(tile, m), min(tile, cols)), BF16), pltpu.SemaphoreType.DMA((2,))],
        compiler_params=params(16),
        cost_estimate=cost(2 * count * slots * m * cols, 2 * count * m * cols),
    )(left, right, *after)


def gather_ctx(mine, n):
    return [lax.ppermute(mine, "ctx", shift(n, s)) for s in range(1, n)]


def exchange(received, exp_count):
    others = jnp.stack(received)
    return others, [lax.ppermute(others, "exp", shift(exp_count, dx)) for dx in range(1, exp_count)]


def siblings(parts, offset):
    pieces, arrays = [], []
    for dx, part in enumerate(parts):
        pieces += [(dx, 0, offset), (dx, 1, offset)]
        arrays += [part, lax.ppermute(part, "tp", shift(2, 1))]
    return pieces, arrays


def per_device(tokens, out_grad, expert_ids, gate_weights, gate_matrix, up_matrix, down_matrix):
    n = lax.axis_size("ctx")
    exp_count = lax.axis_size("exp")
    x = lax.axis_index("exp")
    c = lax.axis_index("tp")
    local_count, depth, hidden_units = gate_matrix.shape
    experts = local_count * exp_count
    block, _ = tokens.shape
    width = depth // (exp_count * 2)
    slots = n * CAP
    here = jnp.stack([x, c, (x * 2 + c) * width, 0]).astype(jnp.int32)

    names = jnp.arange(experts, dtype=jnp.int32)[:, None]
    chosen = [expert_ids[:, k][None, :] == names for k in range(expert_ids.shape[1])]
    member = functools.reduce(jnp.logical_or, chosen)
    before = jnp.arange(block)[:, None] <= jnp.arange(block)[None, :]
    order = jnp.dot(member.astype(BF16), before.astype(BF16), preferred_element_type=F32)
    slot = jnp.where(member, order - 1.0, -1.0)
    weight = sum(jnp.where(ch, gate_weights[:, k][None, :], 0.0) for k, ch in enumerate(chosen))
    meta = jnp.concatenate([slot, weight], axis=0)

    half = width // 256 * 128

    def mine(array, offset, size):
        return lax.dynamic_slice_in_dim(array, (x * 2 + c) * width + offset, size, axis=1)

    m = n - 1
    step = hold(gather_ctx(mine(tokens, 0, width), n) + gather_ctx(meta, n), [])
    t_ctx, metas = step[:m], [meta, *step[m:]]
    t_all, t_exp = exchange(t_ctx, exp_count)
    gate_v, up_v, token = fetch(gate_matrix, up_matrix, t_ctx)
    step = hold(gather_ctx(mine(out_grad, 0, half), n) + t_exp, [token])
    g0, t_exp = step[:m], step[m:]
    t_pieces, t_arrays = siblings([t_all, *t_exp], 0)
    g0_all, g0_exp = exchange(g0, exp_count)
    g1 = gather_ctx(mine(out_grad, half, width - half), n)

    tile = min(512, hidden_units)
    flops = 2 * local_count * slots * depth * hidden_units
    dma = pltpu.SemaphoreType.DMA
    stack = lambda cols, dtype: pltpu.HBM((slots, cols), dtype)
    near = lambda shape: pltpu.HBM(shape, BF16)

    def beside(arrays):
        near_enough = n <= 8
        return [pltpu.with_memory_space_constraint(a, VM) if near_enough else a for a in arrays]

    flat = beside([tokens, *t_arrays])
    forward = []
    for local in range(local_count):
        forward.append(pl.pallas_call(
            functools.partial(forward_kernel, n, exp_count, t_pieces, width, tile, local),
            out_shape=(stack(depth, BF16), stack(hidden_units, BF16),
                       stack(hidden_units, BF16), stack(hidden_units, BF16),
                       jax.ShapeDtypeStruct((8, 128), F32)),
            in_specs=[SCALARS] + vmem(n + len(flat) + 2),
            out_specs=hbm(4) + vmem(1),
            scratch_shapes=[VM((slots, depth), BF16), VM((slots, hidden_units), BF16)]
            + [VM((slots, hidden_units), BF16)] * 2
            + [dma((2 + 2 * (hidden_units // tile),))],
            compiler_params=params(16 if n <= 8 else 40),
            cost_estimate=cost(2 * flops // local_count, 0),
        )(here, *metas, *flat, gate_v, up_v))
        if local == 0:
            step = hold(g1 + g0_exp, forward[0][4:])
            g1, g0_exp = step[:m], step[m:]
            g1_all, g1_exp = exchange(g1, exp_count)
    xps, hiddens, acts, dacts, ends = zip(*forward)
    g1_exp = hold(g1_exp, ends[1:])
    g_pieces, g_arrays = siblings([g0_all, *g0_exp], 0)
    more_pieces, more_arrays = siblings([g1_all, *g1_exp], half)
    g_pieces += more_pieces
    g_arrays += more_arrays

    slabs = [(dx, dc) for dx in [*range(1, exp_count), 0] for dc in (1, 0)]
    at = [lax.rem(x + dx, exp_count) * 2 + lax.rem(c + dc, 2) for dx, dc in slabs]
    part = (n, block, width)
    units = (local_count, slots, hidden_units)
    ring = 3
    flat = beside([out_grad, *g_arrays])
    gp, both_grads, xp, hidden, *outs = pl.pallas_call(
        functools.partial(
            backward_kernel, n, exp_count, g_pieces, width, tile, local_count, len(slabs)
        ),
        out_shape=[VM((local_count, slots, depth), BF16), VM((local_count, slots, 2 * hidden_units), BF16)]
        + [VM((local_count, slots, depth), BF16), VM(units, BF16)] + [near(part)] * len(slabs),
        in_specs=[SCALARS] + vmem(n + len(flat)) + hbm(4 * local_count + 3),
        out_specs=vmem(4) + hbm(len(slabs)),
        scratch_shapes=[VM(units, BF16)] * 2
        + [VM((2, *part), BF16)] + [VM((ring, width, 2 * hidden_units), BF16)]
        + [VM((ring, tile, depth), BF16), dma((2, local_count)),
           dma((2, ring)), dma((ring,)), dma((len(slabs),)), dma((2, local_count))],
        compiler_params=params(36 if n <= 8 else 44),
        cost_estimate=cost(3 * flops, 0),
    )(
        jnp.stack([x, c, *at]).astype(jnp.int32), *metas, *flat, *map(far, acts), *map(far, dacts),
        *map(far, xps), *map(far, hiddens),
        far(gate_matrix), far(up_matrix), far(down_matrix),
    )
    outs = dict(zip(slabs, outs))
    tp_sums = {dx: lax.ppermute(outs[dx, 1], "tp", shift(2, 1)) for dx in range(exp_count)}

    def chip_sum(dx, rows):
        return outs[dx, 0][rows].astype(F32) + tp_sums[dx][rows].astype(F32)

    parts = [slice(0, n // 2), slice(n // 2, n)]
    sent = [
        [chip_sum(dx, rows).astype(BF16) for dx in range(1, exp_count)] for rows in parts
    ]
    grad_gate, token = weight_grad(xp, both_grads, 0, hidden_units, sent[0])
    sent[1] = hold(sent[1], [token])
    arrived = [
        [lax.ppermute(a, "exp", shift(exp_count, dx + 1)) for dx, a in enumerate(group)]
        for group in sent
    ]
    final, rounded = None, []
    for k, rows in enumerate(parts):
        total = chip_sum(0, rows)
        for other in arrived[k]:
            total = total + other.astype(F32)
        rounded.append(total.astype(BF16))
        for j in range(total.shape[0]):
            s = rows.start + j + 1
            if s < n:
                term = lax.ppermute(rounded[k][j], "ctx", shift(n, -s)).astype(F32)
            else:
                term = total[j]
            final = term if final is None else final + term
        if k == 0:
            grad_up, token = weight_grad(xp, both_grads, hidden_units, hidden_units, [token, rounded[0]])
            arrived[1] = hold(arrived[1], [token])
    grad_tokens = final.astype(BF16)

    grad_down, _ = weight_grad(hidden, gp, 0, depth, [token, rounded[1]])
    return (grad_gate, grad_up, grad_down, grad_tokens)


def solution(mesh):
    in_specs = (
        P(("groups", "ctx"), None),
        P(("groups", "ctx"), None),
        P(("groups", "ctx"), None),
        P(("groups", "ctx"), None),
        P("exp", None, ("ctx", "tp")),
        P("exp", None, ("ctx", "tp")),
        P("exp", ("ctx", "tp"), None),
    )
    out_specs = (
        P(("groups", "exp"), None, ("ctx", "tp")),
        P(("groups", "exp"), None, ("ctx", "tp")),
        P(("groups", "exp"), ("ctx", "tp"), None),
        P(("groups", "ctx"), ("exp", "tp")),
    )
    return jax.shard_map(
        per_device, mesh=mesh, in_specs=in_specs, out_specs=out_specs, check_vma=False
    )
```
